512 devices in a mesh: slab: 64 (over y_lo, z, core), fsdp: 8 (over x, y_hi).
Axes of the slice: x: 4, y: 8 (y_hi: 2, y_lo: 4; y = y_hi * 4 + y_lo), z: 8, core: 2. Of those that a mesh axis runs over, the one named last changes fastest.
Arguments:
- queries: bfloat16 [14336, 2048], P('slab', 'fsdp'), may hold values from -160 to 160
- key_rows: bfloat16 [14336, 2048], P('slab', 'fsdp'), may hold values from -5 to 5
- value_rows: bfloat16 [14336, 2048], P('slab', 'fsdp'), may hold values from -6 to 6
- extents: int32 [16, 3], P('fsdp'), may hold values from 0 to 1, as said below
- out_weight: bfloat16 [2048, 3072], P('slab', 'fsdp'), may hold values from -6 to 6
- gate_scale: float32 [3072], P('fsdp'), may hold values from 0.5 to 2
Outputs:
- mixed: bfloat16 [14336, 3072], P('slab', 'fsdp')
The draws below stay inside these ranges and needn't reach their ends.
Inputs may be any that keep to these rules, and one draw needn't show every extreme that they name: `extents`: each entry is 0 or 1, and in every draw some head has 1 in all three.
All inputs are finite; a program needn't handle non-finite values.
Results may differ from the reference program's by a relative error of at most 0.011.
Values may be sent and summed in bfloat16 or wider, within the bound.
No kernel may reach another device: no remote copies, remote signals or barrier semaphores. Data moves between devices by JAX's collectives and lax.ppermute only.
A program may use at most 64 MiB of HBM per device.

```python
import math
import jax
import jax.numpy as jnp
from jax import lax

D = 3072
HD = 128
HEADS = 16
TILE = 224
ST = 4
SH = 4
TOKENS = 14336
N_SLAB = 64


def anchor_setup(key):
    common = jnp.clip(jax.random.normal(key, (TOKENS, HEADS * HD), jnp.float32), -5.0, 5.0)
    return common


def draw_key_rows(key, part):
    common = anchor_setup(key)
    return common.astype(jnp.bfloat16)


def draw_queries(key, part):
    key = jax.random.fold_in(key, 11)
    fresh = jnp.clip(jax.random.normal(key, (TOKENS, HEADS * HD), jnp.float32), -5.0, 5.0)
    return fresh.astype(jnp.bfloat16)


def draw_extents(key, part):
    key = jax.random.fold_in(key, 3)
    reaches = jax.random.randint(key, (HEADS, 3), 0, 2)
    chosen = jax.random.randint(jax.random.fold_in(key, 1), (), 0, HEADS)
    return jnp.where(jnp.arange(HEADS)[:, None] == chosen, 1, reaches).astype(jnp.int32)


def steps_of(key, dims, pieces, low, high):
    factor_of, own = 1.0, jax.random.fold_in(key, 6)
    for axis_at, blocks in pieces:
        draws = jnp.exp(jax.random.uniform(jax.random.fold_in(own, axis_at), (blocks,), jnp.float32, low / len(pieces), high / len(pieces)))
        factor_of = factor_of * jnp.repeat(draws, dims[axis_at] // blocks).reshape([-1 if axis == axis_at else 1 for axis in range(len(dims))])
    return factor_of


def centred(rng, extent, deviation, limit, pieces=(), kind=jnp.bfloat16):
    values = deviation * jax.random.normal(rng, extent, jnp.float32)
    if pieces:
        values = values * steps_of(rng, extent, pieces, -0.22, 0.18)
    return jnp.clip(values, -limit, limit).astype(kind)


def setup_inputs(seed: int = 0) -> dict:
    arg_keys = jax.random.split(jax.random.key(seed), 7)
    queries = draw_queries(jax.random.fold_in(arg_keys[6], 71), 0)
    key_rows = draw_key_rows(jax.random.fold_in(arg_keys[6], 71), 0)
    value_rows = centred(arg_keys[2], (TOKENS, HEADS * HD), 1.0, 6.0, ((0, 64), (1, 8)))
    extents = draw_extents(jax.random.fold_in(arg_keys[6], 71), 0)
    out_weight = centred(arg_keys[4], (HEADS * HD, D), 1.0, 6.0, ((0, 64), (1, 8)))
    gate_scale = jnp.clip(0.5 + 1.5 * jax.random.uniform(arg_keys[5], (D,), jnp.float32) ** steps_of(arg_keys[5], (D,), ((0, 8),), -0.2, 0.2), 0.5, 2.0)
    return {"queries": queries, "key_rows": key_rows, "value_rows": value_rows, "extents": extents, "out_weight": out_weight, "gate_scale": gate_scale}


def reference(queries, key_rows, value_rows, extents, out_weight, gate_scale):
    width_groups = N_SLAB // (ST * SH)
    query_grid = queries.reshape(N_SLAB, TILE, HEADS, HD)
    padding = ((1, 1), (1, 1), (1, 1), (0, 0), (0, 0), (0, 0))
    key_grid = jnp.pad(key_rows.reshape(ST, SH, width_groups, TILE, HEADS, HD), padding)
    value_grid = jnp.pad(value_rows.reshape(ST, SH, width_groups, TILE, HEADS, HD), padding)
    steps_list = [(ts, hs, ws) for ts in (-1, 0, 1) for hs in (-1, 0, 1) for ws in (-1, 0, 1)]

    def one_slab(slab_index):
        time_pos = slab_index // (SH * width_groups)
        height_pos = slab_index // width_groups % SH
        width_pos = slab_index % width_groups
        query_slab = query_grid[slab_index].astype(jnp.float32)
        key_parts = []
        value_parts = []
        mask_parts = []
        for time_step, height_step, width_step in steps_list:
            key_parts.append(key_grid[time_pos + 1 + time_step, height_pos + 1 + height_step, width_pos + 1 + width_step])
            value_parts.append(value_grid[time_pos + 1 + time_step, height_pos + 1 + height_step, width_pos + 1 + width_step])
            valid = (time_pos + time_step >= 0) & (time_pos + time_step < ST) & (height_pos + height_step >= 0) & (height_pos + height_step < SH) & (width_pos + width_step >= 0) & (width_pos + width_step < width_groups)
            head_ok = (abs(time_step) <= extents[:, 0]) & (abs(height_step) <= extents[:, 1]) & (abs(width_step) <= extents[:, 2]) & valid
            mask_parts.append(jnp.broadcast_to(head_ok[:, None, None], (HEADS, TILE, TILE)))
        key_all = jnp.concatenate(key_parts, axis=0).astype(jnp.float32)
        value_all = jnp.concatenate(value_parts, axis=0).astype(jnp.float32)
        mask_all = jnp.concatenate(mask_parts, axis=2)
        scores = jnp.einsum('qhd,khd->hqk', query_slab, key_all) * (1.0 / math.sqrt(HD))
        scores = jnp.where(mask_all, scores, -jnp.inf)
        largest = lax.optimization_barrier(jnp.max(scores, axis=2, keepdims=True))
        weights = jnp.exp(scores - largest)
        totals = lax.optimization_barrier(jnp.sum(weights, axis=2))
        rounded = lax.optimization_barrier(weights.astype(jnp.bfloat16)).astype(jnp.float32)
        summed = jnp.einsum('hqk,khd->qhd', rounded, value_all)
        attended = summed / jnp.transpose(totals)[:, :, None]
        return attended.astype(jnp.bfloat16).reshape(TILE, HEADS * HD)
    attended = lax.map(one_slab, jnp.arange(N_SLAB, dtype=jnp.int32)).reshape(N_SLAB * TILE, HEADS * HD)
    projection = jnp.dot(attended, out_weight, preferred_element_type=jnp.float32)
    return (projection * gate_scale[None, :]).astype(jnp.bfloat16)
```

```python
import functools
import math

import jax
import jax.numpy as jnp
from jax import lax
from jax.experimental import pallas as pl
from jax.experimental.pallas import tpu as pltpu
from jax.sharding import Mesh
from jax.sharding import PartitionSpec as P

HD = 128
ROWS = 224
STATE = HD + 8
SCALE = math.log2(math.e) / math.sqrt(HD)
ROW_AXES = ("t", "u", "w", "c")
COL_AXES = ("x", "h")
VMEM_LIMIT = 32 * 1024 * 1024


def passed_along(value, axis, steps):
    count = lax.axis_size(axis)
    return lax.ppermute(
        value, axis, [(i, i + steps) for i in range(count) if 0 <= i + steps < count]
    )


def exchanged(value, axis):
    return lax.ppermute(value, axis, [(0, 1), (1, 0)])


def online_update(state_ref, tile, queries, keys, values):
    scores = lax.dot_general(
        keys, queries, (((1,), (1,)), ((), ())), preferred_element_type=jnp.float32
    )
    old_max = state_ref[tile, HD : HD + 1, :]
    new_max = jnp.maximum(old_max, jnp.max(scores, axis=0, keepdims=True))
    factor = jnp.exp2((old_max - new_max) * SCALE)
    weights = jnp.exp2((scores - new_max) * SCALE)
    total = state_ref[tile, HD + 1 : HD + 2, :] * factor + jnp.sum(weights, axis=0, keepdims=True)
    added = lax.dot_general(
        values,
        weights.astype(jnp.bfloat16),
        (((0,), (0,)), ((), ())),
        preferred_element_type=jnp.float32,
    )
    state_ref[tile, 0:HD, :] = state_ref[tile, 0:HD, :] * factor + added
    state_ref[tile, HD : HD + 1, :] = new_max
    state_ref[tile, HD + 1 : HD + 2, :] = total


def attend_kernel(blocks, tiles, first, *refs):
    flags_ref, q_ref = refs[0], refs[1]
    kv_refs = refs[2 : 2 + blocks]
    state_ref = refs[-1]
    if first:
        state_ref[...] = jnp.zeros(state_ref.shape, jnp.float32)
        state_ref[:, HD : HD + 1, :] = jnp.full((len(tiles), 1, ROWS), -jnp.inf, jnp.float32)
    else:
        state_ref[...] = refs[2 + blocks][...]
    wide = flags_ref[0] > 0
    facing = flags_ref[1]
    for b in range(blocks):
        kv_ref = kv_refs[b]
        valid = flags_ref[2 + b] > 0

        @pl.when(valid & wide)
        def _():
            for at, tile in enumerate(tiles):
                if tile < 2:
                    online_update(
                        state_ref, at, q_ref[tile], kv_ref[:, 0:HD], kv_ref[:, HD : 2 * HD]
                    )
                else:
                    rows = pl.ds(pl.multiple_of(facing * ROWS, 16), ROWS)
                    online_update(
                        state_ref, at, q_ref[tile], kv_ref[rows, 0:HD], kv_ref[rows, HD : 2 * HD]
                    )

        @pl.when(valid & jnp.logical_not(wide))
        def _():
            for at, tile in enumerate(tiles):
                if tile < 2:
                    rows = pl.ds(tile * ROWS, ROWS)
                    online_update(
                        state_ref, at, q_ref[tile], kv_ref[rows, 0:HD], kv_ref[rows, HD : 2 * HD]
                    )


def attend(flags, queries, key_values, tiles, state=None):
    blocks = len(key_values)
    vmem = pl.BlockSpec(memory_space=pltpu.VMEM)
    operands = [flags, queries, *key_values]
    if state is not None:
        operands.append(state)
    pairs = blocks * sum(2 if tile < 2 else 1 for tile in tiles)
    return pl.pallas_call(
        functools.partial(attend_kernel, blocks, tiles, state is None),
        out_shape=jax.ShapeDtypeStruct((len(tiles), STATE, ROWS), jnp.float32),
        in_specs=[pl.BlockSpec(memory_space=pltpu.SMEM)] + [vmem] * (len(operands) - 1),
        out_specs=vmem,
        compiler_params=pltpu.CompilerParams(vmem_limit_bytes=VMEM_LIMIT),
        cost_estimate=pl.CostEstimate(
            flops=pairs * ROWS * ROWS * HD * 4,
            bytes_accessed=blocks * 4 * ROWS * HD * 2,
            transcendentals=pairs * ROWS * ROWS,
        ),
    )(*operands)


def finish_kernel(flags_ref, own_ref, part_ref, out_ref):
    facing = flags_ref[1]
    for tile in range(2):
        own_max = own_ref[tile, HD : HD + 1, :]
        own_sum = own_ref[tile, HD + 1 : HD + 2, :]
        own = own_ref[tile, 0:HD, :]

        @pl.when(facing == tile)
        def _():
            part_max = part_ref[0, HD : HD + 1, :]
            both_max = jnp.maximum(own_max, part_max)
            own_factor = jnp.exp2((own_max - both_max) * SCALE)
            part_factor = jnp.exp2((part_max - both_max) * SCALE)
            both_sum = own_sum * own_factor + part_ref[0, HD + 1 : HD + 2, :] * part_factor
            both = own * own_factor + part_ref[0, 0:HD, :] * part_factor
            out_ref[tile] = jnp.transpose(both / both_sum).astype(jnp.bfloat16)

        @pl.when(facing != tile)
        def _():
            out_ref[tile] = jnp.transpose(own / own_sum).astype(jnp.bfloat16)


def finish(flags, own, part):
    vmem = pl.BlockSpec(memory_space=pltpu.VMEM)
    return pl.pallas_call(
        finish_kernel,
        out_shape=jax.ShapeDtypeStruct((2, ROWS, HD), jnp.bfloat16),
        in_specs=[pl.BlockSpec(memory_space=pltpu.SMEM), vmem, vmem],
        out_specs=vmem,
        compiler_params=pltpu.CompilerParams(vmem_limit_bytes=VMEM_LIMIT),
    )(flags, own, part)


def project_kernel(groups, order_ref, rows_ref, weight_ref, gate_ref, out_ref):
    total = jnp.zeros(out_ref.shape, jnp.float32)
    for x in range(groups):
        for slot in range(4):
            head = x * 4 + (slot ^ order_ref[0])
            weight = weight_ref[pl.ds(pl.multiple_of(head * HD, HD), HD), :]
            total += jnp.dot(
                rows_ref[x, slot], weight, preferred_element_type=jnp.float32
            )
    out_ref[...] = (total * gate_ref[...]).astype(jnp.bfloat16)


def project(order, rows, weight, gate):
    vmem = pl.BlockSpec(memory_space=pltpu.VMEM)
    return pl.pallas_call(
        functools.partial(project_kernel, rows.shape[0]),
        out_shape=jax.ShapeDtypeStruct((rows.shape[2], weight.shape[1]), jnp.bfloat16),
        in_specs=[pl.BlockSpec(memory_space=pltpu.SMEM), vmem, vmem, vmem],
        out_specs=vmem,
        compiler_params=pltpu.CompilerParams(vmem_limit_bytes=VMEM_LIMIT),
    )(order, rows, weight, gate)


def gathered_weight(out_weight, core):
    mine = lax.all_gather(out_weight, ("u", "w"), axis=0, tiled=False)
    mine = lax.all_gather(mine, "t", axis=0, tiled=False)
    other = exchanged(mine, "c")
    first = jnp.where(core == 0, mine, other)
    second = jnp.where(core == 0, other, mine)
    return jnp.stack([first, second], axis=2).reshape(-1, out_weight.shape[1])


def local(queries, key_rows, value_rows, extents, out_weight, gate_scale):
    time_pos, height_pos, width_pair = (lax.axis_index(a) for a in ("t", "u", "w"))
    core, high = lax.axis_index("c"), lax.axis_index("h")

    def split(value):
        kept = jnp.where(core == 0, value[:, :HD], value[:, HD:])
        given = jnp.where(core == 0, value[:, HD:], value[:, :HD])
        return kept, given

    parts = [split(v) for v in (key_rows, value_rows, queries)]
    kept = jnp.concatenate([p[0] for p in parts], axis=1)
    given = jnp.concatenate([p[1] for p in parts], axis=1)
    taken = exchanged(given, "c")
    both = jnp.stack([kept, taken])
    own_kv = both[:, :, : 2 * HD].reshape(2 * ROWS, 2 * HD)
    own_q = both[:, :, 2 * HD :]

    reach = jnp.where(core == 0, extents[0], extents[1])
    facing = (1 - width_pair) ^ core

    def flags(steps):
        ok = [
            (abs(ts) <= reach[0])
            & (abs(us) <= reach[1])
            & (time_pos + ts >= 0)
            & (time_pos + ts < 4)
            & (height_pos + us >= 0)
            & (height_pos + us < 4)
            for ts, us in steps
        ]
        return jnp.stack([(reach[2] > 0).astype(jnp.int32), facing] + [o.astype(jnp.int32) for o in ok])

    up = {us: passed_along(own_kv, "u", -us) for us in (-1, 1)}
    along = {ts: passed_along(own_kv, "t", -ts) for ts in (-1, 1)}
    facing_q = exchanged(lax.dynamic_index_in_dim(own_q, facing, 0, keepdims=True), "w")
    all_q = jnp.concatenate([own_q, facing_q])
    corners = {(ts, us): passed_along(up[us], "t", -ts) for us in (-1, 1) for ts in (-1, 1)}

    state = attend(flags([(0, 0)]), all_q, [own_kv], (0, 1, 2))
    state = attend(
        flags([(0, -1), (0, 1), (-1, 0), (1, 0)]),
        all_q,
        [up[-1], up[1], along[-1], along[1]],
        (0, 1, 2),
        state,
    )
    steps = [(ts, us) for us in (-1, 1) for ts in (-1, 1)]
    last = [corners[s] for s in steps]
    part = attend(flags(steps), all_q, last, (2,), state[2:])
    back = exchanged(part, "w")
    own = attend(flags(steps), all_q, last, (0, 1), state[:2])
    attended = finish(flags([]), own, back)

    swapped = exchanged(attended[1], "c")
    across = exchanged(attended[0], "h")
    crossed = lax.ppermute(attended[1], ("c", "h"), [(0, 3), (3, 0), (1, 2), (2, 1)])
    four = jnp.stack([attended[0], swapped, across, crossed])
    rows = lax.all_gather(four, "x", axis=0, tiled=False)
    weight = gathered_weight(out_weight, core)
    order = (2 * high + core).reshape(1).astype(jnp.int32)
    return project(order, rows, weight, gate_scale[None, :])


def solution(mesh):
    fine = Mesh(mesh.devices.reshape(4, 4, 2, 2, 4, 2), ROW_AXES + COL_AXES)
    in_specs = (
        P(ROW_AXES, COL_AXES),
        P(ROW_AXES, COL_AXES),
        P(ROW_AXES, COL_AXES),
        P(COL_AXES, None),
        P(ROW_AXES, COL_AXES),
        P(COL_AXES),
    )
    return jax.shard_map(
        local, mesh=fine, in_specs=in_specs, out_specs=P(ROW_AXES, COL_AXES), check_vma=False
    )
```

```python
import functools
import math

import jax
import jax.numpy as jnp
from jax import lax
from jax.experimental import pallas as pl
from jax.experimental.pallas import tpu as pltpu
from jax.sharding import Mesh
from jax.sharding import PartitionSpec as P

HD = 128
ROWS = 224
LANES = 256
STATE = HD + 8
SCALE = math.log2(math.e) / math.sqrt(HD)
ROW_AXES = ("t", "u", "w", "c")
COL_AXES = ("x", "h")
VMEM_LIMIT = 32 * 1024 * 1024


def swapped(value, axis, flip):
    count = lax.axis_size(axis)
    return lax.ppermute(value, axis, [(i, i ^ flip) for i in range(count)])


def middle_swapped(value, axis):
    return lax.ppermute(value, axis, [(1, 2), (2, 1)])


def joined_kernel(*refs):
    start = 0
    for ref in refs[:-1]:
        refs[-1][start : start + ref.shape[0]] = ref[...]
        start += ref.shape[0]


def joined(*parts):
    vmem = pl.BlockSpec(memory_space=pltpu.VMEM)
    first = parts[0]
    rows = sum(p.shape[0] for p in parts)
    return pl.pallas_call(
        joined_kernel,
        out_shape=jax.ShapeDtypeStruct((rows, *first.shape[1:]), first.dtype),
        in_specs=[vmem] * len(parts),
        out_specs=vmem,
        compiler_params=pltpu.CompilerParams(vmem_limit_bytes=VMEM_LIMIT),
    )(*parts)


def beside_kernel(left_ref, right_ref, out_ref, sems):
    width = left_ref.shape[1]
    copies = [
        pltpu.make_async_copy(ref, out_ref.at[:, pl.ds(at * width, width)], sems.at[at])
        for at, ref in enumerate((left_ref, right_ref))
    ]
    for copy in copies:
        copy.start()
    for copy in copies:
        copy.wait()


def beside(left, right):
    return pl.pallas_call(
        beside_kernel,
        out_shape=jax.ShapeDtypeStruct((left.shape[0], 2 * left.shape[1]), left.dtype),
        in_specs=[pl.BlockSpec(memory_space=pl.ANY)] * 2,
        out_specs=pl.BlockSpec(memory_space=pltpu.VMEM),
        scratch_shapes=[pltpu.SemaphoreType.DMA((2,))],
    )(left, right)


def online_update(state_ref, head, lanes, queries, keys, values, first, last_ok):
    scores = lax.dot_general(
        keys, queries, (((1,), (1,)), ((), ())), preferred_element_type=jnp.float32
    )
    if last_ok is not None:
        spare = 2 * ROWS
        scores = jnp.concatenate(
            [scores[:spare], scores[spare:] + jnp.where(last_ok, 0.0, -jnp.inf)]
        )
    new_max = jnp.max(scores, axis=0, keepdims=True)
    if not first:
        old_max = state_ref[head, HD : HD + 1, lanes]
        new_max = jnp.maximum(old_max, new_max)
        factor = jnp.exp2((old_max - new_max) * SCALE)
    weights = jnp.exp2((scores - new_max) * SCALE)
    total = jnp.sum(weights, axis=0, keepdims=True)
    added = lax.dot_general(
        values,
        weights.astype(jnp.bfloat16),
        (((0,), (0,)), ((), ())),
        preferred_element_type=jnp.float32,
    )
    if not first:
        added = state_ref[head, 0:HD, lanes] * factor + added
        total = state_ref[head, HD + 1 : HD + 2, lanes] * factor + total
    state_ref[head, 0:HD, lanes] = added
    state_ref[head, HD : HD + 1, lanes] = new_max
    state_ref[head, HD + 1 : HD + 2, lanes] = total


def attend_kernel(low, high, stage, pos_ref, ext_ref, *refs):
    tiles = high - low
    first = stage == 0
    if first:
        q_refs, (kv_ref, state_ref, q_ref) = refs[:tiles], refs[tiles:]
        for tile in range(tiles):
            q_ref[tile * LANES : tile * LANES + ROWS, :] = q_refs[tile][...]
            q_ref[tile * LANES + ROWS : (tile + 1) * LANES, :] = jnp.zeros(
                (LANES - ROWS, 2 * HD), jnp.bfloat16
            )
        state_ref[...] = jnp.zeros(state_ref.shape, jnp.float32)
        state_ref[:, HD : HD + 1, :] = jnp.full((2, 1, tiles * LANES), -jnp.inf, jnp.float32)
    else:
        q_ref, kv_ref, old_ref, state_ref = refs
        state_ref[...] = old_ref[:, :, low * LANES : high * LANES]
    time_pos, height_pos = pos_ref[0], pos_ref[1]
    inner_t = ((time_pos == 1) | (time_pos == 2)).astype(jnp.int32)
    inner_u = (height_pos == 1) | (height_pos == 2)

    def one_head(head, _):
        reach_t, reach_u, reach_w = (ext_ref[head, i] for i in range(3))
        gate = (1, reach_t, reach_t * inner_t)[stage]
        head_lanes = pl.ds(pl.multiple_of(head * HD, HD), HD)
        value_lanes = pl.ds(pl.multiple_of((head + 2) * HD, HD), HD)
        for tall in (0, 1):
            for wide in (0, 1):
                if (low > 0 and not wide) or (high == 1 and wide):
                    continue
                right = high if wide else 1
                chosen = (reach_u == tall) & (gate > 0)
                if high > 1:
                    chosen &= reach_w == wide

                @pl.when(chosen)
                def _(tall=tall, right=right):
                    rows = slice(0, 3 * ROWS if tall else ROWS)
                    online_update(
                        state_ref,
                        head,
                        slice(0, (right - low) * LANES),
                        q_ref[low * LANES : right * LANES, head_lanes],
                        kv_ref[rows, head_lanes],
                        kv_ref[rows, value_lanes],
                        first,
                        inner_u if tall else None,
                    )

        return 0

    lax.fori_loop(0, 2, one_head, 0)


def attend(pos, extents, queries, low, high, stage, key_values, state=None):
    tiles = high - low
    smem = pl.BlockSpec(memory_space=pltpu.SMEM)
    vmem = pl.BlockSpec(memory_space=pltpu.VMEM)
    out = jax.ShapeDtypeStruct((2, STATE, tiles * LANES), jnp.float32)
    if stage == 0:
        operands = [*queries, key_values]
        out = (out, jax.ShapeDtypeStruct((tiles * LANES, 2 * HD), jnp.bfloat16))
    else:
        operands = [queries, key_values, state]
    pairs = 3 * tiles * 2
    return pl.pallas_call(
        functools.partial(attend_kernel, low, high, stage),
        out_shape=out,
        in_specs=[smem, smem] + [vmem] * len(operands),
        out_specs=(vmem, vmem) if stage == 0 else vmem,
        compiler_params=pltpu.CompilerParams(vmem_limit_bytes=VMEM_LIMIT),
        cost_estimate=pl.CostEstimate(
            flops=pairs * ROWS * ROWS * HD * 4,
            bytes_accessed=12 * ROWS * HD * 2,
            transcendentals=pairs * ROWS * ROWS,
        ),
    )(pos, extents, *operands)


def finish_kernel(pos_ref, own_ref, core_ref, face_ref, out_ref):
    faces = pos_ref[2] != pos_ref[3]
    for head in range(2):
        maxes = [r[head, HD : HD + 1, :] for r in (own_ref, core_ref, face_ref)]
        maxes[2] = jnp.where(faces, maxes[2], -jnp.inf)
        top = jnp.maximum(jnp.maximum(maxes[0], maxes[1]), maxes[2])
        factors = [jnp.exp2((m - top) * SCALE) for m in maxes]
        total = sum(
            r[head, HD + 1 : HD + 2, :] * f for r, f in zip((own_ref, core_ref, face_ref), factors)
        )
        summed = sum(r[head, 0:HD, :] * f for r, f in zip((own_ref, core_ref, face_ref), factors))
        rows = jnp.transpose(summed / total)
        out_ref[:, head * HD : (head + 1) * HD] = rows[:ROWS].astype(jnp.bfloat16)


def finish(pos, own, from_core, from_face):
    vmem = pl.BlockSpec(memory_space=pltpu.VMEM)
    return pl.pallas_call(
        finish_kernel,
        out_shape=jax.ShapeDtypeStruct((ROWS, 2 * HD), jnp.bfloat16),
        in_specs=[pl.BlockSpec(memory_space=pltpu.SMEM), vmem, vmem, vmem],
        out_specs=vmem,
        compiler_params=pltpu.CompilerParams(vmem_limit_bytes=VMEM_LIMIT),
    )(pos, own, from_core, from_face)


def arrange_kernel(pos_ref, mine_ref, other_ref, out_ref):
    time_pos, height_pos, width_pair, core = (pos_ref[i] for i in range(4))
    depth = mine_ref.shape[1]
    for flip_c, ref in enumerate((mine_ref, other_ref)):

        def one_block(at, _, ref=ref, flip_c=flip_c):
            t = time_pos ^ (2 * (at & 1)) ^ ((at >> 3) & 1)
            u = height_pos ^ ((at >> 1) & 1) ^ (3 * ((at >> 2) & 1))
            w = width_pair ^ ((at >> 4) & 1)
            to = ((t * 4 + u) * 2 + w) * 2 + (core ^ flip_c)
            out_ref[pl.ds(pl.multiple_of(to * depth, depth), depth), :] = ref[at]
            return 0

        lax.fori_loop(0, mine_ref.shape[0], one_block, 0, unroll=4)


def arranged_weight(pos, mine, other):
    vmem = pl.BlockSpec(memory_space=pltpu.VMEM)
    return pl.pallas_call(
        arrange_kernel,
        out_shape=jax.ShapeDtypeStruct(
            (2 * mine.shape[0] * mine.shape[1], mine.shape[2]), mine.dtype
        ),
        in_specs=[pl.BlockSpec(memory_space=pltpu.SMEM), vmem, vmem],
        out_specs=vmem,
        compiler_params=pltpu.CompilerParams(vmem_limit_bytes=VMEM_LIMIT),
    )(pos, mine, other)


def project_kernel(groups, pos_ref, rows_ref, weight_ref, gate_ref, out_ref):
    depth = rows_ref.shape[3]
    total = jnp.zeros(out_ref.shape, jnp.float32)
    for x in range(groups):
        for slot in range(2):
            start = (x * 2 + (slot ^ pos_ref[4])) * depth
            weight = weight_ref[pl.ds(pl.multiple_of(start, depth), depth), :]
            total += jnp.dot(rows_ref[x, slot], weight, preferred_element_type=jnp.float32)
    out_ref[...] = (total * gate_ref[...]).astype(jnp.bfloat16)


def project(pos, rows, weight, gate):
    vmem = pl.BlockSpec(memory_space=pltpu.VMEM)
    return pl.pallas_call(
        functools.partial(project_kernel, rows.shape[0]),
        out_shape=jax.ShapeDtypeStruct((rows.shape[2], weight.shape[1]), jnp.bfloat16),
        in_specs=[pl.BlockSpec(memory_space=pltpu.SMEM), vmem, vmem, vmem],
        out_specs=vmem,
        compiler_params=pltpu.CompilerParams(vmem_limit_bytes=VMEM_LIMIT),
    )(pos, rows, weight, gate)


def after(value, other):
    return lax.optimization_barrier((value, other))[0]


def local(queries, key_rows, value_rows, extents, out_weight, gate_scale):
    pos = jnp.stack([lax.axis_index(a) for a in ("t", "u", "w", "c", "h")])

    own_kv = beside(key_rows, value_rows)
    up = swapped(own_kv, "u", 1)
    down = middle_swapped(own_kv, "u")
    facing = [(1, 2), (2, 1)]
    tiles_q = [
        queries,
        swapped(queries, "c", 1),
        lax.ppermute(queries, ("w", "c"), facing),
    ]
    weight = out_weight[None]
    weight_t = swapped(weight, "t", 2)

    up, tiles_q, weight_t = lax.optimization_barrier((up, tiles_q, weight_t))
    near = joined(own_kv, up, down)
    early = swapped(near, "t", 1)
    late = middle_swapped(near, "t")
    weight, weight_t, near = lax.optimization_barrier((weight, weight_t, near))
    weight = joined(weight, weight_t)
    weight_u = swapped(weight, "u", 1)
    state, all_q = attend(pos, extents, tiles_q, 0, 3, 0, near)
    weight = joined(weight, after(weight_u, state))
    state, weight = lax.optimization_barrier((state, weight))
    weight_u = swapped(weight, "u", 3)

    state = attend(pos, extents, all_q, 0, 3, 1, early, state)
    given = attend(pos, extents, all_q, 1, 3, 2, late, state)
    state, given, weight_u = lax.optimization_barrier((state, given, weight_u))
    from_core = swapped(given[:, :, :LANES], "c", 1)
    from_face = lax.ppermute(given[:, :, LANES:], ("w", "c"), facing)
    weight = joined(weight, weight_u)
    weight_t = swapped(weight, "t", 1)
    own = attend(pos, extents, all_q, 0, 1, 2, late, state)
    attended = finish(pos, own, from_core, from_face)

    across = swapped(attended, "h", 1)
    weight = joined(weight, after(weight_t, attended))
    weight_w = swapped(weight, "w", 1)
    rows = lax.all_gather(joined(attended[None], across[None]), "x", axis=0, tiled=False)
    weight = joined(weight, after(weight_w, rows))
    weight = arranged_weight(pos, weight, swapped(weight, "c", 1))
    return project(pos, rows, weight, gate_scale[None, :])


def solution(mesh):
    fine = Mesh(mesh.devices.reshape(4, 4, 2, 2, 4, 2), ROW_AXES + COL_AXES)
    in_specs = (
        P(ROW_AXES, COL_AXES),
        P(ROW_AXES, COL_AXES),
        P(ROW_AXES, COL_AXES),
        P(COL_AXES, None),
        P(ROW_AXES, COL_AXES),
        P(COL_AXES),
    )
    return jax.shard_map(
        local, mesh=fine, in_specs=in_specs, out_specs=P(ROW_AXES, COL_AXES), check_vma=False
    )
```

```python
import functools
import math

import jax
import jax.numpy as jnp
from jax import lax
from jax.experimental import pallas as pl
from jax.experimental.pallas import tpu as pltpu
from jax.sharding import Mesh
from jax.sharding import PartitionSpec as P

HD = 128
ROWS = 224
LANES = 256
STATE = HD + 8
SCALE = math.log2(math.e) / math.sqrt(HD)
ROW_AXES = ("t", "u", "w", "c")
COL_AXES = ("x", "h")
VMEM_LIMIT = 32 * 1024 * 1024


def swapped(value, axis, flip):
    count = lax.axis_size(axis)
    return lax.ppermute(value, axis, [(i, i ^ flip) for i in range(count)])


def middle_swapped(value, axis):
    return lax.ppermute(value, axis, [(1, 2), (2, 1)])


def joined_kernel(*refs):
    start = 0
    for ref in refs[:-1]:
        refs[-1][start : start + ref.shape[0]] = ref[...]
        start += ref.shape[0]


def joined(*parts):
    vmem = pl.BlockSpec(memory_space=pltpu.VMEM)
    first = parts[0]
    rows = sum(p.shape[0] for p in parts)
    return pl.pallas_call(
        joined_kernel,
        out_shape=jax.ShapeDtypeStruct((rows, *first.shape[1:]), first.dtype),
        in_specs=[vmem] * len(parts),
        out_specs=vmem,
        compiler_params=pltpu.CompilerParams(vmem_limit_bytes=VMEM_LIMIT),
    )(*parts)


def beside_kernel(left_ref, right_ref, out_ref, sems):
    width = left_ref.shape[1]
    copies = [
        pltpu.make_async_copy(ref, out_ref.at[:, pl.ds(at * width, width)], sems.at[at])
        for at, ref in enumerate((left_ref, right_ref))
    ]
    for copy in copies:
        copy.start()
    for copy in copies:
        copy.wait()


def beside(left, right):
    return pl.pallas_call(
        beside_kernel,
        out_shape=jax.ShapeDtypeStruct((left.shape[0], 2 * left.shape[1]), left.dtype),
        in_specs=[pl.BlockSpec(memory_space=pl.ANY)] * 2,
        out_specs=pl.BlockSpec(memory_space=pltpu.VMEM),
        scratch_shapes=[pltpu.SemaphoreType.DMA((2,))],
    )(left, right)


def online_update(state_ref, head, lanes, queries, keys, values, first, last_ok):
    scores = lax.dot_general(
        keys, queries, (((1,), (1,)), ((), ())), preferred_element_type=jnp.float32
    )
    if last_ok is not None:
        spare = 2 * ROWS
        scores = jnp.concatenate(
            [scores[:spare], scores[spare:] + jnp.where(last_ok, 0.0, -jnp.inf)]
        )
    new_max = jnp.max(scores, axis=0, keepdims=True)
    if not first:
        old_max = state_ref[head, HD : HD + 1, lanes]
        new_max = jnp.maximum(old_max, new_max)
        factor = jnp.exp2((old_max - new_max) * SCALE)
    weights = jnp.exp2((scores - new_max) * SCALE)
    total = jnp.sum(weights, axis=0, keepdims=True)
    added = lax.dot_general(
        values,
        weights.astype(jnp.bfloat16),
        (((0,), (0,)), ((), ())),
        preferred_element_type=jnp.float32,
    )
    if not first:
        added = state_ref[head, 0:HD, lanes] * factor + added
        total = state_ref[head, HD + 1 : HD + 2, lanes] * factor + total
    state_ref[head, 0:HD, lanes] = added
    state_ref[head, HD : HD + 1, lanes] = new_max
    state_ref[head, HD + 1 : HD + 2, lanes] = total


def attend_kernel(low, high, stage, pos_ref, ext_ref, *refs):
    tiles = high - low
    first = stage == 0
    if first:
        q_refs, (kv_ref, state_ref, q_ref) = refs[:tiles], refs[tiles:]
        for tile in range(tiles):
            q_ref[tile * LANES : tile * LANES + ROWS, :] = q_refs[tile][...]
            q_ref[tile * LANES + ROWS : (tile + 1) * LANES, :] = jnp.zeros(
                (LANES - ROWS, 2 * HD), jnp.bfloat16
            )
        state_ref[...] = jnp.zeros(state_ref.shape, jnp.float32)
        state_ref[:, HD : HD + 1, :] = jnp.full((2, 1, tiles * LANES), -jnp.inf, jnp.float32)
    else:
        q_ref, kv_ref, old_ref, state_ref = refs
        state_ref[...] = old_ref[:, :, low * LANES : high * LANES]
    time_pos, height_pos = pos_ref[0], pos_ref[1]
    inner_t = ((time_pos == 1) | (time_pos == 2)).astype(jnp.int32)
    inner_u = (height_pos == 1) | (height_pos == 2)

    def one_head(head, _):
        reach_t, reach_u, reach_w = (ext_ref[head, i] for i in range(3))
        gate = (1, reach_t, reach_t * inner_t)[stage]
        head_lanes = pl.ds(pl.multiple_of(head * HD, HD), HD)
        value_lanes = pl.ds(pl.multiple_of((head + 2) * HD, HD), HD)
        for tall in (0, 1):
            for wide in (0, 1):
                if (low > 0 and not wide) or (high == 1 and wide):
                    continue
                right = high if wide else 1
                chosen = (reach_u == tall) & (gate > 0)
                if high > 1:
                    chosen &= reach_w == wide

                @pl.when(chosen)
                def _(tall=tall, right=right):
                    rows = slice(0, 3 * ROWS if tall else ROWS)
                    online_update(
                        state_ref,
                        head,
                        slice(0, (right - low) * LANES),
                        q_ref[low * LANES : right * LANES, head_lanes],
                        kv_ref[rows, head_lanes],
                        kv_ref[rows, value_lanes],
                        first,
                        inner_u if tall else None,
                    )

        return 0

    lax.fori_loop(0, 2, one_head, 0)


def attend(pos, extents, queries, low, high, stage, key_values, state=None):
    tiles = high - low
    smem = pl.BlockSpec(memory_space=pltpu.SMEM)
    vmem = pl.BlockSpec(memory_space=pltpu.VMEM)
    out = jax.ShapeDtypeStruct((2, STATE, tiles * LANES), jnp.float32)
    if stage == 0:
        operands = [*queries, key_values]
        out = (out, jax.ShapeDtypeStruct((tiles * LANES, 2 * HD), jnp.bfloat16))
    else:
        operands = [queries, key_values, state]
    pairs = 3 * tiles * 2
    return pl.pallas_call(
        functools.partial(attend_kernel, low, high, stage),
        out_shape=out,
        in_specs=[smem, smem] + [vmem] * len(operands),
        out_specs=(vmem, vmem) if stage == 0 else vmem,
        compiler_params=pltpu.CompilerParams(vmem_limit_bytes=VMEM_LIMIT),
        cost_estimate=pl.CostEstimate(
            flops=pairs * ROWS * ROWS * HD * 4,
            bytes_accessed=12 * ROWS * HD * 2,
            transcendentals=pairs * ROWS * ROWS,
        ),
    )(pos, extents, *operands)


def finish_kernel(pos_ref, own_ref, core_ref, face_ref, out_ref):
    faces = pos_ref[2] != pos_ref[3]
    for head in range(2):
        maxes = [r[head, HD : HD + 1, :] for r in (own_ref, core_ref, face_ref)]
        maxes[2] = jnp.where(faces, maxes[2], -jnp.inf)
        top = jnp.maximum(jnp.maximum(maxes[0], maxes[1]), maxes[2])
        factors = [jnp.exp2((m - top) * SCALE) for m in maxes]
        total = sum(
            r[head, HD + 1 : HD + 2, :] * f for r, f in zip((own_ref, core_ref, face_ref), factors)
        )
        summed = sum(r[head, 0:HD, :] * f for r, f in zip((own_ref, core_ref, face_ref), factors))
        rows = jnp.transpose(summed / total)
        out_ref[:, head * HD : (head + 1) * HD] = rows[:ROWS].astype(jnp.bfloat16)


def finish(pos, own, from_core, from_face):
    vmem = pl.BlockSpec(memory_space=pltpu.VMEM)
    return pl.pallas_call(
        finish_kernel,
        out_shape=jax.ShapeDtypeStruct((ROWS, 2 * HD), jnp.bfloat16),
        in_specs=[pl.BlockSpec(memory_space=pltpu.SMEM), vmem, vmem, vmem],
        out_specs=vmem,
        compiler_params=pltpu.CompilerParams(vmem_limit_bytes=VMEM_LIMIT),
    )(pos, own, from_core, from_face)


def arrange_kernel(pos_ref, mine_ref, other_ref, out_ref):
    time_pos, height_pos, width_pair, core = (pos_ref[i] for i in range(4))
    depth = mine_ref.shape[1]
    for flip_c, ref in enumerate((mine_ref, other_ref)):

        def one_block(at, _, ref=ref, flip_c=flip_c):
            t = time_pos ^ (2 * (at & 1)) ^ ((at >> 3) & 1)
            u = height_pos ^ ((at >> 1) & 1) ^ (3 * ((at >> 2) & 1))
            w = width_pair ^ ((at >> 4) & 1)
            to = ((t * 4 + u) * 2 + w) * 2 + (core ^ flip_c)
            out_ref[pl.ds(pl.multiple_of(to * depth, depth), depth), :] = ref[at]
            return 0

        lax.fori_loop(0, mine_ref.shape[0], one_block, 0, unroll=4)


def arranged_weight(pos, mine, other):
    vmem = pl.BlockSpec(memory_space=pltpu.VMEM)
    return pl.pallas_call(
        arrange_kernel,
        out_shape=jax.ShapeDtypeStruct(
            (2 * mine.shape[0] * mine.shape[1], mine.shape[2]), mine.dtype
        ),
        in_specs=[pl.BlockSpec(memory_space=pltpu.SMEM), vmem, vmem],
        out_specs=vmem,
        compiler_params=pltpu.CompilerParams(vmem_limit_bytes=VMEM_LIMIT),
    )(pos, mine, other)


def project_kernel(groups, pos_ref, rows_ref, weight_ref, gate_ref, out_ref):
    depth = rows_ref.shape[3]
    total = jnp.zeros(out_ref.shape, jnp.float32)
    for x in range(groups):
        for slot in range(2):
            start = (x * 2 + (slot ^ pos_ref[4])) * depth
            weight = weight_ref[pl.ds(pl.multiple_of(start, depth), depth), :]
            total += jnp.dot(rows_ref[x, slot], weight, preferred_element_type=jnp.float32)
    out_ref[...] = (total * gate_ref[...]).astype(jnp.bfloat16)


def project(pos, rows, weight, gate):
    vmem = pl.BlockSpec(memory_space=pltpu.VMEM)
    return pl.pallas_call(
        functools.partial(project_kernel, rows.shape[0]),
        out_shape=jax.ShapeDtypeStruct((rows.shape[2], weight.shape[1]), jnp.bfloat16),
        in_specs=[pl.BlockSpec(memory_space=pltpu.SMEM), vmem, vmem, vmem],
        out_specs=vmem,
        compiler_params=pltpu.CompilerParams(vmem_limit_bytes=VMEM_LIMIT),
    )(pos, rows, weight, gate)


def after(value, other):
    return lax.optimization_barrier((value, other))[0]


def local(queries, key_rows, value_rows, extents, out_weight, gate_scale):
    pos = jnp.stack([lax.axis_index(a) for a in ("t", "u", "w", "c", "h")])

    own_kv = beside(key_rows, value_rows)
    up = swapped(own_kv, "u", 1)
    down = middle_swapped(own_kv, "u")
    facing = [(1, 2), (2, 1)]
    tiles_q = [
        queries,
        swapped(queries, "c", 1),
        lax.ppermute(queries, ("w", "c"), facing),
    ]
    weight = out_weight[None]
    weight = joined(weight, swapped(weight, "t", 2))

    down, tiles_q, weight = lax.optimization_barrier((down, tiles_q, weight))
    near = joined(own_kv, up, down)
    early = swapped(near, "t", 1)
    late = middle_swapped(near, "t")
    weight, near = lax.optimization_barrier((weight, near))
    weight_u = swapped(weight, "u", 1)
    state, all_q = attend(pos, extents, tiles_q, 0, 3, 0, near)
    weight = joined(weight, after(weight_u, state))
    state, weight = lax.optimization_barrier((state, weight))
    weight_u = swapped(weight, "u", 3)

    state = attend(pos, extents, all_q, 0, 3, 1, early, state)
    given = attend(pos, extents, all_q, 1, 3, 2, late, state)
    state, given, weight_u = lax.optimization_barrier((state, given, weight_u))
    from_core = swapped(given[:, :, :LANES], "c", 1)
    from_face = lax.ppermute(given[:, :, LANES:], ("w", "c"), facing)
    weight = joined(weight, weight_u)
    weight_t = swapped(weight, "t", 1)
    own = attend(pos, extents, all_q, 0, 1, 2, late, state)
    attended = finish(pos, own, after(from_core, own), from_face)

    across = swapped(attended, "h", 1)
    weight = joined(weight, after(weight_t, attended))
    weight_w = swapped(weight, "w", 1)
    rows = lax.all_gather(joined(attended[None], across[None]), "x", axis=0, tiled=False)
    weight = joined(weight, after(weight_w, rows))
    weight = arranged_weight(pos, weight, swapped(weight, "c", 1))
    return project(pos, rows, weight, gate_scale[None, :])


def solution(mesh):
    fine = Mesh(mesh.devices.reshape(4, 4, 2, 2, 4, 2), ROW_AXES + COL_AXES)
    in_specs = (
        P(ROW_AXES, COL_AXES),
        P(ROW_AXES, COL_AXES),
        P(ROW_AXES, COL_AXES),
        P(COL_AXES, None),
        P(ROW_AXES, COL_AXES),
        P(COL_AXES),
    )
    return jax.shard_map(
        local, mesh=fine, in_specs=in_specs, out_specs=P(ROW_AXES, COL_AXES), check_vma=False
    )
```

```python
import functools
import math

import jax
import jax.numpy as jnp
from jax import lax
from jax.experimental import pallas as pl
from jax.experimental.pallas import tpu as pltpu
from jax.sharding import Mesh
from jax.sharding import PartitionSpec as P

HD = 128
ROWS = 224
LANES = 256
STATE = HD + 8
SCALE = math.log2(math.e) / math.sqrt(HD)
ROW_AXES = ("t", "u", "w", "c")
COL_AXES = ("x", "h")
VMEM_LIMIT = 32 * 1024 * 1024


def swapped(value, axis, flip):
    count = lax.axis_size(axis)
    return lax.ppermute(value, axis, [(i, i ^ flip) for i in range(count)])


def middle_swapped(value, axis):
    return lax.ppermute(value, axis, [(1, 2), (2, 1)])


def joined_kernel(*refs):
    start = 0
    for ref in refs[:-1]:
        refs[-1][start : start + ref.shape[0]] = ref[...]
        start += ref.shape[0]


def joined(*parts):
    vmem = pl.BlockSpec(memory_space=pltpu.VMEM)
    first = parts[0]
    rows = sum(p.shape[0] for p in parts)
    return pl.pallas_call(
        joined_kernel,
        out_shape=jax.ShapeDtypeStruct((rows, *first.shape[1:]), first.dtype),
        in_specs=[vmem] * len(parts),
        out_specs=vmem,
        compiler_params=pltpu.CompilerParams(vmem_limit_bytes=VMEM_LIMIT),
    )(*parts)


def staged_kernel(key_ref, value_ref, q_ref, weight_ref, kv_out, q_out, weight_out, sems):
    width = key_ref.shape[1]
    pairs = [
        (key_ref, kv_out.at[:, pl.ds(0, width)]),
        (value_ref, kv_out.at[:, pl.ds(width, width)]),
        (weight_ref, weight_out.at[0]),
        (q_ref, q_out),
    ]
    copies = [
        pltpu.make_async_copy(src, dst, sems.at[at]) for at, (src, dst) in enumerate(pairs)
    ]
    for copy in copies:
        copy.start()
    for copy in copies:
        copy.wait()


def staged(keys, values, queries, weight):
    vmem = pl.BlockSpec(memory_space=pltpu.VMEM)
    rows, width = keys.shape
    return pl.pallas_call(
        staged_kernel,
        out_shape=(
            jax.ShapeDtypeStruct((rows, 2 * width), keys.dtype),
            jax.ShapeDtypeStruct(queries.shape, queries.dtype),
            jax.ShapeDtypeStruct((1, *weight.shape), weight.dtype),
        ),
        in_specs=[pl.BlockSpec(memory_space=pl.ANY)] * 4,
        out_specs=(vmem, vmem, vmem),
        scratch_shapes=[pltpu.SemaphoreType.DMA((4,))],
    )(keys, values, queries, weight)


def online_update(state_ref, head, lanes, queries, keys, values, first, last_ok):
    scores = lax.dot_general(
        keys, queries, (((1,), (1,)), ((), ())), preferred_element_type=jnp.float32
    )
    if last_ok is not None:
        spare = 2 * ROWS
        scores = jnp.concatenate(
            [scores[:spare], scores[spare:] + jnp.where(last_ok, 0.0, -jnp.inf)]
        )
    new_max = jnp.max(scores, axis=0, keepdims=True)
    if not first:
        old_max = state_ref[head, HD : HD + 1, lanes]
        new_max = jnp.maximum(old_max, new_max)
        factor = jnp.exp2((old_max - new_max) * SCALE)
    weights = jnp.exp2((scores - new_max) * SCALE)
    total = jnp.sum(weights, axis=0, keepdims=True)
    added = lax.dot_general(
        values,
        weights.astype(jnp.bfloat16),
        (((0,), (0,)), ((), ())),
        preferred_element_type=jnp.float32,
    )
    if not first:
        added = state_ref[head, 0:HD, lanes] * factor + added
        total = state_ref[head, HD + 1 : HD + 2, lanes] * factor + total
    state_ref[head, 0:HD, lanes] = added
    state_ref[head, HD : HD + 1, lanes] = new_max
    state_ref[head, HD + 1 : HD + 2, lanes] = total


def attend_kernel(low, high, stage, pos_ref, ext_ref, *refs):
    tiles = high - low
    first = stage == 0
    if first:
        q_refs, (kv_ref, state_ref, q_ref) = refs[:tiles], refs[tiles:]
        for tile in range(tiles):
            q_ref[tile * LANES : tile * LANES + ROWS, :] = q_refs[tile][...]
            q_ref[tile * LANES + ROWS : (tile + 1) * LANES, :] = jnp.zeros(
                (LANES - ROWS, 2 * HD), jnp.bfloat16
            )
        state_ref[...] = jnp.zeros(state_ref.shape, jnp.float32)
        state_ref[:, HD : HD + 1, :] = jnp.full((2, 1, tiles * LANES), -jnp.inf, jnp.float32)
    else:
        q_ref, kv_ref, old_ref, state_ref = refs
        state_ref[...] = old_ref[:, :, low * LANES : high * LANES]
    time_pos, height_pos = pos_ref[0], pos_ref[1]
    inner_t = ((time_pos == 1) | (time_pos == 2)).astype(jnp.int32)
    inner_u = (height_pos == 1) | (height_pos == 2)

    def one_head(head, _):
        reach_t, reach_u, reach_w = (ext_ref[head, i] for i in range(3))
        gate = (1, reach_t, reach_t * inner_t)[stage]
        head_lanes = pl.ds(pl.multiple_of(head * HD, HD), HD)
        value_lanes = pl.ds(pl.multiple_of((head + 2) * HD, HD), HD)
        for tall in (0, 1):
            for wide in (0, 1):
                if (low > 0 and not wide) or (high == 1 and wide):
                    continue
                right = high if wide else 1
                chosen = (reach_u == tall) & (gate > 0)
                if high > 1:
                    chosen &= reach_w == wide

                @pl.when(chosen)
                def _(tall=tall, right=right):
                    rows = slice(0, 3 * ROWS if tall else ROWS)
                    online_update(
                        state_ref,
                        head,
                        slice(0, (right - low) * LANES),
                        q_ref[low * LANES : right * LANES, head_lanes],
                        kv_ref[rows, head_lanes],
                        kv_ref[rows, value_lanes],
                        first,
                        inner_u if tall else None,
                    )

        return 0

    lax.fori_loop(0, 2, one_head, 0)


def attend(pos, extents, queries, low, high, stage, key_values, state=None):
    tiles = high - low
    smem = pl.BlockSpec(memory_space=pltpu.SMEM)
    vmem = pl.BlockSpec(memory_space=pltpu.VMEM)
    out = jax.ShapeDtypeStruct((2, STATE, tiles * LANES), jnp.float32)
    if stage == 0:
        operands = [*queries, key_values]
        out = (out, jax.ShapeDtypeStruct((tiles * LANES, 2 * HD), jnp.bfloat16))
    else:
        operands = [queries, key_values, state]
    pairs = 3 * tiles * 2
    return pl.pallas_call(
        functools.partial(attend_kernel, low, high, stage),
        out_shape=out,
        in_specs=[smem, smem] + [vmem] * len(operands),
        out_specs=(vmem, vmem) if stage == 0 else vmem,
        compiler_params=pltpu.CompilerParams(vmem_limit_bytes=VMEM_LIMIT),
        cost_estimate=pl.CostEstimate(
            flops=pairs * ROWS * ROWS * HD * 4,
            bytes_accessed=12 * ROWS * HD * 2,
            transcendentals=pairs * ROWS * ROWS,
        ),
    )(pos, extents, *operands)


def finish_kernel(pos_ref, own_ref, core_ref, face_ref, out_ref):
    faces = pos_ref[2] != pos_ref[3]
    for head in range(2):
        maxes = [r[head, HD : HD + 1, :] for r in (own_ref, core_ref, face_ref)]
        maxes[2] = jnp.where(faces, maxes[2], -jnp.inf)
        top = jnp.maximum(jnp.maximum(maxes[0], maxes[1]), maxes[2])
        factors = [jnp.exp2((m - top) * SCALE) for m in maxes]
        total = sum(
            r[head, HD + 1 : HD + 2, :] * f for r, f in zip((own_ref, core_ref, face_ref), factors)
        )
        summed = sum(r[head, 0:HD, :] * f for r, f in zip((own_ref, core_ref, face_ref), factors))
        rows = jnp.transpose(summed / total)
        out_ref[:, head * HD : (head + 1) * HD] = rows[:ROWS].astype(jnp.bfloat16)


def finish(pos, own, from_core, from_face):
    vmem = pl.BlockSpec(memory_space=pltpu.VMEM)
    return pl.pallas_call(
        finish_kernel,
        out_shape=jax.ShapeDtypeStruct((ROWS, 2 * HD), jnp.bfloat16),
        in_specs=[pl.BlockSpec(memory_space=pltpu.SMEM), vmem, vmem, vmem],
        out_specs=vmem,
        compiler_params=pltpu.CompilerParams(vmem_limit_bytes=VMEM_LIMIT),
    )(pos, own, from_core, from_face)


def arrange_kernel(pos_ref, mine_ref, other_ref, out_ref):
    time_pos, height_pos, width_pair, core = (pos_ref[i] for i in range(4))
    depth = mine_ref.shape[1]
    for flip_c, ref in enumerate((mine_ref, other_ref)):

        def one_block(at, _, ref=ref, flip_c=flip_c):
            t = time_pos ^ (2 * (at & 1)) ^ ((at >> 3) & 1)
            u = height_pos ^ ((at >> 1) & 1) ^ (3 * ((at >> 2) & 1))
            w = width_pair ^ ((at >> 4) & 1)
            to = ((t * 4 + u) * 2 + w) * 2 + (core ^ flip_c)
            out_ref[pl.ds(pl.multiple_of(to * depth, depth), depth), :] = ref[at]
            return 0

        lax.fori_loop(0, mine_ref.shape[0], one_block, 0, unroll=4)


def arranged_weight(pos, mine, other):
    vmem = pl.BlockSpec(memory_space=pltpu.VMEM)
    return pl.pallas_call(
        arrange_kernel,
        out_shape=jax.ShapeDtypeStruct(
            (2 * mine.shape[0] * mine.shape[1], mine.shape[2]), mine.dtype
        ),
        in_specs=[pl.BlockSpec(memory_space=pltpu.SMEM), vmem, vmem],
        out_specs=vmem,
        compiler_params=pltpu.CompilerParams(vmem_limit_bytes=VMEM_LIMIT),
    )(pos, mine, other)


def project_kernel(groups, pos_ref, rows_ref, weight_ref, gate_ref, out_ref):
    depth = rows_ref.shape[3]
    total = jnp.zeros(out_ref.shape, jnp.float32)
    for x in range(groups):
        for slot in range(2):
            start = (x * 2 + (slot ^ pos_ref[4])) * depth
            weight = weight_ref[pl.ds(pl.multiple_of(start, depth), depth), :]
            total += jnp.dot(rows_ref[x, slot], weight, preferred_element_type=jnp.float32)
    out_ref[...] = (total * gate_ref[...]).astype(jnp.bfloat16)


def project(pos, rows, weight, gate):
    vmem = pl.BlockSpec(memory_space=pltpu.VMEM)
    return pl.pallas_call(
        functools.partial(project_kernel, rows.shape[0]),
        out_shape=jax.ShapeDtypeStruct((rows.shape[2], weight.shape[1]), jnp.bfloat16),
        in_specs=[pl.BlockSpec(memory_space=pltpu.SMEM), vmem, vmem, vmem],
        out_specs=vmem,
        compiler_params=pltpu.CompilerParams(vmem_limit_bytes=VMEM_LIMIT),
    )(pos, rows, weight, gate)


def after(value, other):
    return lax.optimization_barrier((value, other))[0]


def local(queries, key_rows, value_rows, extents, out_weight, gate_scale):
    pos = jnp.stack([lax.axis_index(a) for a in ("t", "u", "w", "c", "h")])

    own_kv, queries, weight = staged(key_rows, value_rows, queries, out_weight)
    up = swapped(own_kv, "u", 1)
    down = middle_swapped(own_kv, "u")
    facing = [(1, 2), (2, 1)]
    tiles_q = [
        queries,
        swapped(queries, "c", 1),
        lax.ppermute(queries, ("w", "c"), facing),
    ]
    weight = joined(weight, swapped(weight, "t", 2))

    down, tiles_q, weight = lax.optimization_barrier((down, tiles_q, weight))
    near = joined(own_kv, up, down)
    early = swapped(near, "t", 1)
    late = middle_swapped(near, "t")
    weight, near = lax.optimization_barrier((weight, near))
    weight_u = swapped(weight, "u", 1)
    state, all_q = attend(pos, extents, tiles_q, 0, 3, 0, near)
    weight = joined(weight, after(weight_u, state))
    state, weight = lax.optimization_barrier((state, weight))
    weight_u = swapped(weight, "u", 3)

    state = attend(pos, extents, all_q, 0, 3, 1, early, state)
    given = attend(pos, extents, all_q, 1, 3, 2, late, state)
    state, given, weight_u = lax.optimization_barrier((state, given, weight_u))
    from_core = swapped(given[:, :, :LANES], "c", 1)
    from_face = lax.ppermute(given[:, :, LANES:], ("w", "c"), facing)
    weight = joined(weight, weight_u)
    weight_t = swapped(weight, "t", 1)
    own = attend(pos, extents, all_q, 0, 1, 2, late, state)
    attended = finish(pos, own, after(from_core, own), from_face)

    across = swapped(attended, "h", 1)
    weight = joined(weight, after(weight_t, attended))
    weight_w = swapped(weight, "w", 1)
    rows = lax.all_gather(joined(attended[None], across[None]), "x", axis=0, tiled=False)
    weight = joined(weight, after(weight_w, rows))
    weight = arranged_weight(pos, weight, swapped(weight, "c", 1))
    return project(pos, rows, weight, gate_scale[None, :])


def solution(mesh):
    fine = Mesh(mesh.devices.reshape(4, 4, 2, 2, 4, 2), ROW_AXES + COL_AXES)
    in_specs = (
        P(ROW_AXES, COL_AXES),
        P(ROW_AXES, COL_AXES),
        P(ROW_AXES, COL_AXES),
        P(COL_AXES, None),
        P(ROW_AXES, COL_AXES),
        P(COL_AXES),
    )
    return jax.shard_map(
        local, mesh=fine, in_specs=in_specs, out_specs=P(ROW_AXES, COL_AXES), check_vma=False
    )
```

```python
import functools
import math

import jax
import jax.numpy as jnp
from jax import lax
from jax.experimental import pallas as pl
from jax.experimental.pallas import tpu as pltpu
from jax.sharding import Mesh
from jax.sharding import PartitionSpec as P

HD = 128
ROWS = 224
LANES = 256
STATE = HD + 8
SCALE = math.log2(math.e) / math.sqrt(HD)
ROW_AXES = ("t", "u", "w", "c")
COL_AXES = ("x", "h")
VMEM_LIMIT = 32 * 1024 * 1024


def swapped(value, axis, flip):
    count = lax.axis_size(axis)
    return lax.ppermute(value, axis, [(i, i ^ flip) for i in range(count)])


def middle_swapped(value, axis):
    return lax.ppermute(value, axis, [(1, 2), (2, 1)])


def joined_kernel(*refs):
    start = 0
    for ref in refs[:-1]:
        refs[-1][start : start + ref.shape[0]] = ref[...]
        start += ref.shape[0]


def joined(*parts):
    vmem = pl.BlockSpec(memory_space=pltpu.VMEM)
    first = parts[0]
    rows = sum(p.shape[0] for p in parts)
    return pl.pallas_call(
        joined_kernel,
        out_shape=jax.ShapeDtypeStruct((rows, *first.shape[1:]), first.dtype),
        in_specs=[vmem] * len(parts),
        out_specs=vmem,
        compiler_params=pltpu.CompilerParams(vmem_limit_bytes=VMEM_LIMIT),
    )(*parts)


def staged_kernel(key_ref, value_ref, q_ref, weight_ref, kv_out, q_out, weight_out, sems):
    width = key_ref.shape[1]
    pairs = [
        (key_ref, kv_out.at[:, pl.ds(0, width)]),
        (value_ref, kv_out.at[:, pl.ds(width, width)]),
        (weight_ref, weight_out.at[0]),
        (q_ref, q_out),
    ]
    copies = [
        pltpu.make_async_copy(src, dst, sems.at[at]) for at, (src, dst) in enumerate(pairs)
    ]
    for copy in copies:
        copy.start()
    for copy in copies:
        copy.wait()


def staged(keys, values, queries, weight):
    vmem = pl.BlockSpec(memory_space=pltpu.VMEM)
    rows, width = keys.shape
    return pl.pallas_call(
        staged_kernel,
        out_shape=(
            jax.ShapeDtypeStruct((rows, 2 * width), keys.dtype),
            jax.ShapeDtypeStruct(queries.shape, queries.dtype),
            jax.ShapeDtypeStruct((1, *weight.shape), weight.dtype),
        ),
        in_specs=[pl.BlockSpec(memory_space=pl.ANY)] * 4,
        out_specs=(vmem, vmem, vmem),
        scratch_shapes=[pltpu.SemaphoreType.DMA((4,))],
        compiler_params=pltpu.CompilerParams(vmem_limit_bytes=VMEM_LIMIT),
    )(keys, values, queries, weight)


def online_update(state_ref, head, lanes, queries, keys, values, first, last_ok):
    scores = lax.dot_general(
        keys, queries, (((1,), (1,)), ((), ())), preferred_element_type=jnp.float32
    )
    if last_ok is not None:
        spare = 2 * ROWS
        scores = jnp.concatenate(
            [scores[:spare], scores[spare:] + jnp.where(last_ok, 0.0, -jnp.inf)]
        )
    new_max = jnp.max(scores, axis=0, keepdims=True)
    if not first:
        old_max = state_ref[head, HD : HD + 1, lanes]
        new_max = jnp.maximum(old_max, new_max)
        factor = jnp.exp2((old_max - new_max) * SCALE)
    weights = jnp.exp2((scores - new_max) * SCALE)
    total = jnp.sum(weights, axis=0, keepdims=True)
    added = lax.dot_general(
        values,
        weights.astype(jnp.bfloat16),
        (((0,), (0,)), ((), ())),
        preferred_element_type=jnp.float32,
    )
    if not first:
        added = state_ref[head, 0:HD, lanes] * factor + added
        total = state_ref[head, HD + 1 : HD + 2, lanes] * factor + total
    state_ref[head, 0:HD, lanes] = added
    state_ref[head, HD : HD + 1, lanes] = new_max
    state_ref[head, HD + 1 : HD + 2, lanes] = total


def attend_kernel(low, high, stage, pos_ref, ext_ref, *refs):
    tiles = high - low
    first = stage == 0
    if first:
        q_refs, (kv_ref, state_ref, q_ref) = refs[:tiles], refs[tiles:]
        for tile in range(tiles):
            q_ref[tile * LANES : tile * LANES + ROWS, :] = q_refs[tile][...]
            q_ref[tile * LANES + ROWS : (tile + 1) * LANES, :] = jnp.zeros(
                (LANES - ROWS, 2 * HD), jnp.bfloat16
            )
        state_ref[...] = jnp.zeros(state_ref.shape, jnp.float32)
        state_ref[:, HD : HD + 1, :] = jnp.full((2, 1, tiles * LANES), -jnp.inf, jnp.float32)
    else:
        q_ref, kv_ref, old_ref, state_ref = refs
        state_ref[...] = old_ref[:, :, low * LANES : high * LANES]
    time_pos, height_pos = pos_ref[0], pos_ref[1]
    inner_t = ((time_pos == 1) | (time_pos == 2)).astype(jnp.int32)
    inner_u = (height_pos == 1) | (height_pos == 2)

    def one_head(head, _):
        reach_t, reach_u, reach_w = (ext_ref[head, i] for i in range(3))
        gate = (1, reach_t, reach_t * inner_t)[stage]
        head_lanes = pl.ds(pl.multiple_of(head * HD, HD), HD)
        value_lanes = pl.ds(pl.multiple_of((head + 2) * HD, HD), HD)
        for tall in (0, 1):
            for wide in (0, 1):
                if (low > 0 and not wide) or (high == 1 and wide):
                    continue
                right = high if wide else 1
                chosen = (reach_u == tall) & (gate > 0)
                if high > 1:
                    chosen &= reach_w == wide

                @pl.when(chosen)
                def _(tall=tall, right=right):
                    rows = slice(0, 3 * ROWS if tall else ROWS)
                    online_update(
                        state_ref,
                        head,
                        slice(0, (right - low) * LANES),
                        q_ref[low * LANES : right * LANES, head_lanes],
                        kv_ref[rows, head_lanes],
                        kv_ref[rows, value_lanes],
                        first,
                        inner_u if tall else None,
                    )

        return 0

    lax.fori_loop(0, 2, one_head, 0)


def attend(pos, extents, queries, low, high, stage, key_values, state=None):
    tiles = high - low
    smem = pl.BlockSpec(memory_space=pltpu.SMEM)
    vmem = pl.BlockSpec(memory_space=pltpu.VMEM)
    out = jax.ShapeDtypeStruct((2, STATE, tiles * LANES), jnp.float32)
    if stage == 0:
        operands = [*queries, key_values]
        out = (out, jax.ShapeDtypeStruct((tiles * LANES, 2 * HD), jnp.bfloat16))
    else:
        operands = [queries, key_values, state]
    pairs = 3 * tiles * 2
    return pl.pallas_call(
        functools.partial(attend_kernel, low, high, stage),
        out_shape=out,
        in_specs=[smem, smem] + [vmem] * len(operands),
        out_specs=(vmem, vmem) if stage == 0 else vmem,
        compiler_params=pltpu.CompilerParams(vmem_limit_bytes=VMEM_LIMIT),
        cost_estimate=pl.CostEstimate(
            flops=pairs * ROWS * ROWS * HD * 4,
            bytes_accessed=12 * ROWS * HD * 2,
            transcendentals=pairs * ROWS * ROWS,
        ),
    )(pos, extents, *operands)


def finish_kernel(pos_ref, own_ref, core_ref, face_ref, out_ref):
    faces = pos_ref[2] != pos_ref[3]
    for head in range(2):
        maxes = [r[head, HD : HD + 1, :] for r in (own_ref, core_ref, face_ref)]
        maxes[2] = jnp.where(faces, maxes[2], -jnp.inf)
        top = jnp.maximum(jnp.maximum(maxes[0], maxes[1]), maxes[2])
        factors = [jnp.exp2((m - top) * SCALE) for m in maxes]
        total = sum(
            r[head, HD + 1 : HD + 2, :] * f for r, f in zip((own_ref, core_ref, face_ref), factors)
        )
        summed = sum(r[head, 0:HD, :] * f for r, f in zip((own_ref, core_ref, face_ref), factors))
        rows = jnp.transpose(summed / total)
        out_ref[:, head * HD : (head + 1) * HD] = rows[:ROWS].astype(jnp.bfloat16)


def finish(pos, own, from_core, from_face):
    vmem = pl.BlockSpec(memory_space=pltpu.VMEM)
    return pl.pallas_call(
        finish_kernel,
        out_shape=jax.ShapeDtypeStruct((ROWS, 2 * HD), jnp.bfloat16),
        in_specs=[pl.BlockSpec(memory_space=pltpu.SMEM), vmem, vmem, vmem],
        out_specs=vmem,
        compiler_params=pltpu.CompilerParams(vmem_limit_bytes=VMEM_LIMIT),
    )(pos, own, from_core, from_face)


def arrange_kernel(pos_ref, mine_ref, other_ref, out_ref):
    time_pos, height_pos, width_pair, core = (pos_ref[i] for i in range(4))
    depth = mine_ref.shape[1]
    for flip_c, ref in enumerate((mine_ref, other_ref)):

        def one_block(at, _, ref=ref, flip_c=flip_c):
            t = time_pos ^ (2 * (at & 1)) ^ ((at >> 3) & 1)
            u = height_pos ^ ((at >> 1) & 1) ^ (3 * ((at >> 2) & 1))
            w = width_pair ^ ((at >> 4) & 1)
            to = ((t * 4 + u) * 2 + w) * 2 + (core ^ flip_c)
            out_ref[pl.ds(pl.multiple_of(to * depth, depth), depth), :] = ref[at]
            return 0

        lax.fori_loop(0, mine_ref.shape[0], one_block, 0, unroll=4)


def arranged_weight(pos, mine, other):
    vmem = pl.BlockSpec(memory_space=pltpu.VMEM)
    return pl.pallas_call(
        arrange_kernel,
        out_shape=jax.ShapeDtypeStruct(
            (2 * mine.shape[0] * mine.shape[1], mine.shape[2]), mine.dtype
        ),
        in_specs=[pl.BlockSpec(memory_space=pltpu.SMEM), vmem, vmem],
        out_specs=vmem,
        compiler_params=pltpu.CompilerParams(vmem_limit_bytes=VMEM_LIMIT),
    )(pos, mine, other)


def project_kernel(groups, pos_ref, rows_ref, weight_ref, gate_ref, out_ref):
    depth = rows_ref.shape[3]
    total = jnp.zeros(out_ref.shape, jnp.float32)
    for x in range(groups):
        for slot in range(2):
            start = (x * 2 + (slot ^ pos_ref[4])) * depth
            weight = weight_ref[pl.ds(pl.multiple_of(start, depth), depth), :]
            total += jnp.dot(rows_ref[x, slot], weight, preferred_element_type=jnp.float32)
    out_ref[...] = (total * gate_ref[...]).astype(jnp.bfloat16)


def project(pos, rows, weight, gate):
    vmem = pl.BlockSpec(memory_space=pltpu.VMEM)
    return pl.pallas_call(
        functools.partial(project_kernel, rows.shape[0]),
        out_shape=jax.ShapeDtypeStruct((rows.shape[2], weight.shape[1]), jnp.bfloat16),
        in_specs=[pl.BlockSpec(memory_space=pltpu.SMEM), vmem, vmem, vmem],
        out_specs=vmem,
        compiler_params=pltpu.CompilerParams(vmem_limit_bytes=VMEM_LIMIT),
    )(pos, rows, weight, gate)


def after(value, other):
    return lax.optimization_barrier((value, other))[0]


def local(queries, key_rows, value_rows, extents, out_weight, gate_scale):
    pos = jnp.stack([lax.axis_index(a) for a in ("t", "u", "w", "c", "h")])

    own_kv, queries, weight = staged(key_rows, value_rows, queries, out_weight)
    up = swapped(own_kv, "u", 1)
    down = middle_swapped(own_kv, "u")
    facing = [(1, 2), (2, 1)]
    tiles_q = [
        queries,
        swapped(queries, "c", 1),
        lax.ppermute(queries, ("w", "c"), facing),
    ]
    weight = joined(weight, swapped(weight, "t", 2))

    down, tiles_q, weight = lax.optimization_barrier((down, tiles_q, weight))
    near = joined(own_kv, up, down)
    early = swapped(near, "t", 1)
    late = middle_swapped(near, "t")
    weight, near = lax.optimization_barrier((weight, near))
    weight_u = swapped(weight, "u", 1)
    state, all_q = attend(pos, extents, tiles_q, 0, 3, 0, near)
    weight = joined(weight, after(weight_u, state))
    state, weight = lax.optimization_barrier((state, weight))
    weight_u = swapped(weight, "u", 3)

    state = attend(pos, extents, all_q, 0, 3, 1, early, state)
    given = attend(pos, extents, all_q, 1, 3, 2, late, state)
    state, given, weight_u = lax.optimization_barrier((state, given, weight_u))
    from_core = swapped(given[:, :, :LANES], "c", 1)
    from_face = lax.ppermute(given[:, :, LANES:], ("w", "c"), facing)
    weight = joined(weight, weight_u)
    weight_t = swapped(weight, "t", 1)
    own = attend(pos, extents, all_q, 0, 1, 2, late, state)
    attended = finish(pos, own, after(from_core, own), from_face)

    across = swapped(attended, "h", 1)
    weight = joined(weight, after(weight_t, attended))
    weight_w = swapped(weight, "w", 1)
    rows = lax.all_gather(joined(attended[None], across[None]), "x", axis=0, tiled=False)
    weight = joined(weight, after(weight_w, rows))
    weight = arranged_weight(pos, weight, swapped(weight, "c", 1))
    return project(pos, rows, weight, gate_scale[None, :])


def solution(mesh):
    fine = Mesh(mesh.devices.reshape(4, 4, 2, 2, 4, 2), ROW_AXES + COL_AXES)
    in_specs = (
        P(ROW_AXES, COL_AXES),
        P(ROW_AXES, COL_AXES),
        P(ROW_AXES, COL_AXES),
        P(COL_AXES, None),
        P(ROW_AXES, COL_AXES),
        P(COL_AXES),
    )
    return jax.shard_map(
        local, mesh=fine, in_specs=in_specs, out_specs=P(ROW_AXES, COL_AXES), check_vma=False
    )
```

```python
import functools
import math

import jax
import jax.numpy as jnp
from jax import lax
from jax.experimental import pallas as pl
from jax.experimental.pallas import tpu as pltpu
from jax.sharding import Mesh
from jax.sharding import PartitionSpec as P

HD = 128
ROWS = 224
LANES = 256
STATE = HD + 8
SCALE = math.log2(math.e) / math.sqrt(HD)
ROW_AXES = ("t", "u", "w", "c")
COL_AXES = ("x", "h")
VMEM_LIMIT = 32 * 1024 * 1024


def swapped(value, axis, flip):
    count = lax.axis_size(axis)
    return lax.ppermute(value, axis, [(i, i ^ flip) for i in range(count)])


def middle_swapped(value, axis):
    return lax.ppermute(value, axis, [(1, 2), (2, 1)])


def joined_kernel(*refs):
    start = 0
    for ref in refs[:-1]:
        refs[-1][start : start + ref.shape[0]] = ref[...]
        start += ref.shape[0]


def joined(*parts):
    vmem = pl.BlockSpec(memory_space=pltpu.VMEM)
    first = parts[0]
    rows = sum(p.shape[0] for p in parts)
    return pl.pallas_call(
        joined_kernel,
        out_shape=jax.ShapeDtypeStruct((rows, *first.shape[1:]), first.dtype),
        in_specs=[vmem] * len(parts),
        out_specs=vmem,
        compiler_params=pltpu.CompilerParams(vmem_limit_bytes=VMEM_LIMIT),
    )(*parts)


def beside_kernel(left_ref, right_ref, out_ref, sems):
    width = left_ref.shape[1]
    copies = [
        pltpu.make_async_copy(ref, out_ref.at[:, pl.ds(at * width, width)], sems.at[at])
        for at, ref in enumerate((left_ref, right_ref))
    ]
    for copy in copies:
        copy.start()
    for copy in copies:
        copy.wait()


def beside(left, right):
    return pl.pallas_call(
        beside_kernel,
        out_shape=jax.ShapeDtypeStruct((left.shape[0], 2 * left.shape[1]), left.dtype),
        in_specs=[pl.BlockSpec(memory_space=pl.ANY)] * 2,
        out_specs=pl.BlockSpec(memory_space=pltpu.VMEM),
        scratch_shapes=[pltpu.SemaphoreType.DMA((2,))],
        compiler_params=pltpu.CompilerParams(vmem_limit_bytes=VMEM_LIMIT),
    )(left, right)


def online_update(state_ref, head, lanes, queries, keys, values, first, last_ok):
    scores = lax.dot_general(
        keys, queries, (((1,), (1,)), ((), ())), preferred_element_type=jnp.float32
    )
    if last_ok is not None:
        spare = 2 * ROWS
        scores = jnp.concatenate(
            [scores[:spare], scores[spare:] + jnp.where(last_ok, 0.0, -jnp.inf)]
        )
    new_max = jnp.max(scores, axis=0, keepdims=True)
    if not first:
        old_max = state_ref[head, HD : HD + 1, lanes]
        new_max = jnp.maximum(old_max, new_max)
        factor = jnp.exp2((old_max - new_max) * SCALE)
    weights = jnp.exp2((scores - new_max) * SCALE)
    total = jnp.sum(weights, axis=0, keepdims=True)
    added = lax.dot_general(
        values,
        weights.astype(jnp.bfloat16),
        (((0,), (0,)), ((), ())),
        preferred_element_type=jnp.float32,
    )
    if not first:
        added = state_ref[head, 0:HD, lanes] * factor + added
        total = state_ref[head, HD + 1 : HD + 2, lanes] * factor + total
    state_ref[head, 0:HD, lanes] = added
    state_ref[head, HD : HD + 1, lanes] = new_max
    state_ref[head, HD + 1 : HD + 2, lanes] = total


def attend_kernel(low, high, stage, pos_ref, ext_ref, *refs):
    tiles = high - low
    first = stage == 0
    if first:
        q_refs, (kv_ref, state_ref, q_ref) = refs[:tiles], refs[tiles:]
        for tile in range(tiles):
            q_ref[tile * LANES : tile * LANES + ROWS, :] = q_refs[tile][...]
            q_ref[tile * LANES + ROWS : (tile + 1) * LANES, :] = jnp.zeros(
                (LANES - ROWS, 2 * HD), jnp.bfloat16
            )
        state_ref[...] = jnp.zeros(state_ref.shape, jnp.float32)
        state_ref[:, HD : HD + 1, :] = jnp.full((2, 1, tiles * LANES), -jnp.inf, jnp.float32)
    else:
        q_ref, kv_ref, old_ref, state_ref = refs
        state_ref[...] = old_ref[:, :, low * LANES : high * LANES]
    time_pos, height_pos = pos_ref[0], pos_ref[1]
    inner_t = ((time_pos == 1) | (time_pos == 2)).astype(jnp.int32)
    inner_u = (height_pos == 1) | (height_pos == 2)

    def one_head(head, _):
        reach_t, reach_u, reach_w = (ext_ref[head, i] for i in range(3))
        gate = (1, reach_t, reach_t * inner_t)[stage]
        head_lanes = pl.ds(pl.multiple_of(head * HD, HD), HD)
        value_lanes = pl.ds(pl.multiple_of((head + 2) * HD, HD), HD)
        for tall in (0, 1):
            for wide in (0, 1):
                if (low > 0 and not wide) or (high == 1 and wide):
                    continue
                right = high if wide else 1
                chosen = (reach_u == tall) & (gate > 0)
                if high > 1:
                    chosen &= reach_w == wide

                @pl.when(chosen)
                def _(tall=tall, right=right):
                    rows = slice(0, 3 * ROWS if tall else ROWS)
                    online_update(
                        state_ref,
                        head,
                        slice(0, (right - low) * LANES),
                        q_ref[low * LANES : right * LANES, head_lanes],
                        kv_ref[rows, head_lanes],
                        kv_ref[rows, value_lanes],
                        first,
                        inner_u if tall else None,
                    )

        return 0

    lax.fori_loop(0, 2, one_head, 0)


def attend(pos, extents, queries, low, high, stage, key_values, state=None):
    tiles = high - low
    smem = pl.BlockSpec(memory_space=pltpu.SMEM)
    vmem = pl.BlockSpec(memory_space=pltpu.VMEM)
    out = jax.ShapeDtypeStruct((2, STATE, tiles * LANES), jnp.float32)
    if stage == 0:
        operands = [*queries, key_values]
        out = (out, jax.ShapeDtypeStruct((tiles * LANES, 2 * HD), jnp.bfloat16))
    else:
        operands = [queries, key_values, state]
    pairs = 3 * tiles * 2
    return pl.pallas_call(
        functools.partial(attend_kernel, low, high, stage),
        out_shape=out,
        in_specs=[smem, smem] + [vmem] * len(operands),
        out_specs=(vmem, vmem) if stage == 0 else vmem,
        compiler_params=pltpu.CompilerParams(vmem_limit_bytes=VMEM_LIMIT),
        cost_estimate=pl.CostEstimate(
            flops=pairs * ROWS * ROWS * HD * 4,
            bytes_accessed=12 * ROWS * HD * 2,
            transcendentals=pairs * ROWS * ROWS,
        ),
    )(pos, extents, *operands)


def finish_kernel(pos_ref, own_ref, core_ref, face_ref, out_ref):
    faces = pos_ref[2] != pos_ref[3]
    for head in range(2):
        maxes = [r[head, HD : HD + 1, :] for r in (own_ref, core_ref, face_ref)]
        maxes[2] = jnp.where(faces, maxes[2], -jnp.inf)
        top = jnp.maximum(jnp.maximum(maxes[0], maxes[1]), maxes[2])
        factors = [jnp.exp2((m - top) * SCALE) for m in maxes]
        total = sum(
            r[head, HD + 1 : HD + 2, :] * f for r, f in zip((own_ref, core_ref, face_ref), factors)
        )
        summed = sum(r[head, 0:HD, :] * f for r, f in zip((own_ref, core_ref, face_ref), factors))
        rows = jnp.transpose(summed / total)
        out_ref[:, head * HD : (head + 1) * HD] = rows[:ROWS].astype(jnp.bfloat16)


def finish(pos, own, from_core, from_face):
    vmem = pl.BlockSpec(memory_space=pltpu.VMEM)
    return pl.pallas_call(
        finish_kernel,
        out_shape=jax.ShapeDtypeStruct((ROWS, 2 * HD), jnp.bfloat16),
        in_specs=[pl.BlockSpec(memory_space=pltpu.SMEM), vmem, vmem, vmem],
        out_specs=vmem,
        compiler_params=pltpu.CompilerParams(vmem_limit_bytes=VMEM_LIMIT),
    )(pos, own, from_core, from_face)


def arrange_kernel(pos_ref, mine_ref, other_ref, out_ref):
    time_pos, height_pos, width_pair, core = (pos_ref[i] for i in range(4))
    depth = mine_ref.shape[1]
    for flip_c, ref in enumerate((mine_ref, other_ref)):

        def one_block(at, _, ref=ref, flip_c=flip_c):
            t = time_pos ^ (2 * (at & 1)) ^ ((at >> 3) & 1)
            u = height_pos ^ ((at >> 1) & 1) ^ (3 * ((at >> 2) & 1))
            w = width_pair ^ ((at >> 4) & 1)
            to = ((t * 4 + u) * 2 + w) * 2 + (core ^ flip_c)
            out_ref[pl.ds(pl.multiple_of(to * depth, depth), depth), :] = ref[at]
            return 0

        lax.fori_loop(0, mine_ref.shape[0], one_block, 0, unroll=4)


def arranged_weight(pos, mine, other):
    vmem = pl.BlockSpec(memory_space=pltpu.VMEM)
    return pl.pallas_call(
        arrange_kernel,
        out_shape=jax.ShapeDtypeStruct(
            (2 * mine.shape[0] * mine.shape[1], mine.shape[2]), mine.dtype
        ),
        in_specs=[pl.BlockSpec(memory_space=pltpu.SMEM), vmem, vmem],
        out_specs=vmem,
        compiler_params=pltpu.CompilerParams(vmem_limit_bytes=VMEM_LIMIT),
    )(pos, mine, other)


def project_kernel(groups, pos_ref, rows_ref, weight_ref, gate_ref, out_ref):
    depth = rows_ref.shape[3]
    total = jnp.zeros(out_ref.shape, jnp.float32)
    for x in range(groups):
        for slot in range(2):
            start = (x * 2 + (slot ^ pos_ref[4])) * depth
            weight = weight_ref[pl.ds(pl.multiple_of(start, depth), depth), :]
            total += jnp.dot(rows_ref[x, slot], weight, preferred_element_type=jnp.float32)
    out_ref[...] = (total * gate_ref[...]).astype(jnp.bfloat16)


def project(pos, rows, weight, gate):
    vmem = pl.BlockSpec(memory_space=pltpu.VMEM)
    return pl.pallas_call(
        functools.partial(project_kernel, rows.shape[0]),
        out_shape=jax.ShapeDtypeStruct((rows.shape[2], weight.shape[1]), jnp.bfloat16),
        in_specs=[pl.BlockSpec(memory_space=pltpu.SMEM), vmem, vmem, vmem],
        out_specs=vmem,
        compiler_params=pltpu.CompilerParams(vmem_limit_bytes=VMEM_LIMIT),
    )(pos, rows, weight, gate)


def after(value, other):
    return lax.optimization_barrier((value, other))[0]


def local(queries, key_rows, value_rows, extents, out_weight, gate_scale):
    pos = jnp.stack([lax.axis_index(a) for a in ("t", "u", "w", "c", "h")])

    own_kv = beside(key_rows, value_rows)
    up = swapped(own_kv, "u", 1)
    down = middle_swapped(own_kv, "u")
    facing = [(1, 2), (2, 1)]
    tiles_q = [
        queries,
        swapped(queries, "c", 1),
        lax.ppermute(queries, ("w", "c"), facing),
    ]
    weight = out_weight[None]
    weight = joined(weight, swapped(weight, "t", 2))

    down, tiles_q, weight = lax.optimization_barrier((down, tiles_q, weight))
    near = joined(own_kv, up, down)
    early = swapped(near, "t", 1)
    late = middle_swapped(near, "t")
    weight, near = lax.optimization_barrier((weight, near))
    weight_u = swapped(weight, "u", 1)
    state, all_q = attend(pos, extents, tiles_q, 0, 3, 0, near)
    weight = joined(weight, after(weight_u, state))
    state, weight = lax.optimization_barrier((state, weight))
    weight_u = swapped(weight, "u", 3)

    state = attend(pos, extents, all_q, 0, 3, 1, early, state)
    given = attend(pos, extents, all_q, 1, 3, 2, late, state)
    state, given, weight_u = lax.optimization_barrier((state, given, weight_u))
    from_core = swapped(given[:, :, :LANES], "c", 1)
    from_face = lax.ppermute(given[:, :, LANES:], ("w", "c"), facing)
    weight = joined(weight, weight_u)
    weight_t = swapped(weight, "t", 1)
    own = attend(pos, extents, all_q, 0, 1, 2, late, state)
    attended = finish(pos, own, after(from_core, own), from_face)

    across = swapped(attended, "h", 1)
    weight = joined(weight, after(weight_t, attended))
    weight_w = swapped(weight, "w", 1)
    rows = lax.all_gather(joined(attended[None], across[None]), "x", axis=0, tiled=False)
    weight = joined(weight, after(weight_w, rows))
    weight = arranged_weight(pos, weight, swapped(weight, "c", 1))
    return project(pos, rows, weight, gate_scale[None, :])


def solution(mesh):
    fine = Mesh(mesh.devices.reshape(4, 4, 2, 2, 4, 2), ROW_AXES + COL_AXES)
    in_specs = (
        P(ROW_AXES, COL_AXES),
        P(ROW_AXES, COL_AXES),
        P(ROW_AXES, COL_AXES),
        P(COL_AXES, None),
        P(ROW_AXES, COL_AXES),
        P(COL_AXES),
    )
    return jax.shard_map(
        local, mesh=fine, in_specs=in_specs, out_specs=P(ROW_AXES, COL_AXES), check_vma=False
    )
```

```python
import functools
import math

import jax
import jax.numpy as jnp
from jax import lax
from jax.experimental import pallas as pl
from jax.experimental.pallas import tpu as pltpu
from jax.sharding import Mesh
from jax.sharding import PartitionSpec as P

HD = 128
ROWS = 224
LANES = 256
STATE = HD + 8
SCALE = math.log2(math.e) / math.sqrt(HD)
ROW_AXES = ("t", "u", "w", "c")
COL_AXES = ("x", "h")
VMEM_LIMIT = 32 * 1024 * 1024


def swapped(value, axis, flip):
    count = lax.axis_size(axis)
    return lax.ppermute(value, axis, [(i, i ^ flip) for i in range(count)])


def middle_swapped(value, axis):
    return lax.ppermute(value, axis, [(1, 2), (2, 1)])


def joined_kernel(*refs):
    start = 0
    for ref in refs[:-1]:
        refs[-1][start : start + ref.shape[0]] = ref[...]
        start += ref.shape[0]


def joined(*parts):
    vmem = pl.BlockSpec(memory_space=pltpu.VMEM)
    first = parts[0]
    rows = sum(p.shape[0] for p in parts)
    return pl.pallas_call(
        joined_kernel,
        out_shape=jax.ShapeDtypeStruct((rows, *first.shape[1:]), first.dtype),
        in_specs=[vmem] * len(parts),
        out_specs=vmem,
        compiler_params=pltpu.CompilerParams(vmem_limit_bytes=VMEM_LIMIT),
    )(*parts)


def beside_kernel(left_ref, right_ref, out_ref, sems):
    width = left_ref.shape[1]
    copies = [
        pltpu.make_async_copy(ref, out_ref.at[:, pl.ds(at * width, width)], sems.at[at])
        for at, ref in enumerate((left_ref, right_ref))
    ]
    for copy in copies:
        copy.start()
    for copy in copies:
        copy.wait()


def beside(left, right):
    return pl.pallas_call(
        beside_kernel,
        out_shape=jax.ShapeDtypeStruct((left.shape[0], 2 * left.shape[1]), left.dtype),
        in_specs=[pl.BlockSpec(memory_space=pl.ANY)] * 2,
        out_specs=pl.BlockSpec(memory_space=pltpu.VMEM),
        scratch_shapes=[pltpu.SemaphoreType.DMA((2,))],
        compiler_params=pltpu.CompilerParams(vmem_limit_bytes=VMEM_LIMIT),
    )(left, right)


def online_update(state_ref, head, lanes, queries, keys, values, first, last_ok):
    scores = lax.dot_general(
        keys, queries, (((1,), (1,)), ((), ())), preferred_element_type=jnp.float32
    )
    if last_ok is not None:
        spare = 2 * ROWS
        scores = jnp.concatenate(
            [scores[:spare], scores[spare:] + jnp.where(last_ok, 0.0, -jnp.inf)]
        )
    new_max = jnp.max(scores, axis=0, keepdims=True)
    if not first:
        old_max = state_ref[head, HD : HD + 1, lanes]
        new_max = jnp.maximum(old_max, new_max)
        factor = jnp.exp2((old_max - new_max) * SCALE)
    weights = jnp.exp2((scores - new_max) * SCALE)
    total = jnp.sum(weights, axis=0, keepdims=True)
    added = lax.dot_general(
        values,
        weights.astype(jnp.bfloat16),
        (((0,), (0,)), ((), ())),
        preferred_element_type=jnp.float32,
    )
    if not first:
        added = state_ref[head, 0:HD, lanes] * factor + added
        total = state_ref[head, HD + 1 : HD + 2, lanes] * factor + total
    state_ref[head, 0:HD, lanes] = added
    state_ref[head, HD : HD + 1, lanes] = new_max
    state_ref[head, HD + 1 : HD + 2, lanes] = total


def attend_kernel(low, high, stage, pos_ref, ext_ref, *refs):
    tiles = high - low
    first = stage == 0
    if first:
        q_refs, (kv_ref, state_ref, q_ref) = refs[:tiles], refs[tiles:]
        for tile in range(tiles):
            q_ref[tile * LANES : tile * LANES + ROWS, :] = q_refs[tile][...]
            q_ref[tile * LANES + ROWS : (tile + 1) * LANES, :] = jnp.zeros(
                (LANES - ROWS, 2 * HD), jnp.bfloat16
            )
        state_ref[...] = jnp.zeros(state_ref.shape, jnp.float32)
        state_ref[:, HD : HD + 1, :] = jnp.full((2, 1, tiles * LANES), -jnp.inf, jnp.float32)
    else:
        q_ref, kv_ref, old_ref, state_ref = refs
        state_ref[...] = old_ref[:, :, low * LANES : high * LANES]
    time_pos, height_pos = pos_ref[0], pos_ref[1]
    inner_t = ((time_pos == 1) | (time_pos == 2)).astype(jnp.int32)
    inner_u = (height_pos == 1) | (height_pos == 2)

    def one_head(head, _):
        reach_t, reach_u, reach_w = (ext_ref[head, i] for i in range(3))
        gate = (1, reach_t, reach_t * inner_t)[stage]
        head_lanes = pl.ds(pl.multiple_of(head * HD, HD), HD)
        value_lanes = pl.ds(pl.multiple_of((head + 2) * HD, HD), HD)
        for tall in (0, 1):
            for wide in (0, 1):
                if (low > 0 and not wide) or (high == 1 and wide):
                    continue
                right = high if wide else 1
                chosen = (reach_u == tall) & (gate > 0)
                if high > 1:
                    chosen &= reach_w == wide

                @pl.when(chosen)
                def _(tall=tall, right=right):
                    rows = slice(0, 3 * ROWS if tall else ROWS)
                    online_update(
                        state_ref,
                        head,
                        slice(0, (right - low) * LANES),
                        q_ref[low * LANES : right * LANES, head_lanes],
                        kv_ref[rows, head_lanes],
                        kv_ref[rows, value_lanes],
                        first,
                        inner_u if tall else None,
                    )

        return 0

    lax.fori_loop(0, 2, one_head, 0)


def attend(pos, extents, queries, low, high, stage, key_values, state=None):
    tiles = high - low
    smem = pl.BlockSpec(memory_space=pltpu.SMEM)
    vmem = pl.BlockSpec(memory_space=pltpu.VMEM)
    out = jax.ShapeDtypeStruct((2, STATE, tiles * LANES), jnp.float32)
    if stage == 0:
        operands = [*queries, key_values]
        out = (out, jax.ShapeDtypeStruct((tiles * LANES, 2 * HD), jnp.bfloat16))
    else:
        operands = [queries, key_values, state]
    pairs = 3 * tiles * 2
    return pl.pallas_call(
        functools.partial(attend_kernel, low, high, stage),
        out_shape=out,
        in_specs=[smem, smem] + [vmem] * len(operands),
        out_specs=(vmem, vmem) if stage == 0 else vmem,
        compiler_params=pltpu.CompilerParams(vmem_limit_bytes=VMEM_LIMIT),
        cost_estimate=pl.CostEstimate(
            flops=pairs * ROWS * ROWS * HD * 4,
            bytes_accessed=12 * ROWS * HD * 2,
            transcendentals=pairs * ROWS * ROWS,
        ),
    )(pos, extents, *operands)


def finish_kernel(pos_ref, own_ref, core_ref, face_ref, out_ref):
    faces = pos_ref[2] != pos_ref[3]
    for head in range(2):
        maxes = [r[head, HD : HD + 1, :] for r in (own_ref, core_ref, face_ref)]
        maxes[2] = jnp.where(faces, maxes[2], -jnp.inf)
        top = jnp.maximum(jnp.maximum(maxes[0], maxes[1]), maxes[2])
        factors = [jnp.exp2((m - top) * SCALE) for m in maxes]
        total = sum(
            r[head, HD + 1 : HD + 2, :] * f for r, f in zip((own_ref, core_ref, face_ref), factors)
        )
        summed = sum(r[head, 0:HD, :] * f for r, f in zip((own_ref, core_ref, face_ref), factors))
        rows = jnp.transpose(summed / total)
        out_ref[:, head * HD : (head + 1) * HD] = rows[:ROWS].astype(jnp.bfloat16)


def finish(pos, own, from_core, from_face):
    vmem = pl.BlockSpec(memory_space=pltpu.VMEM)
    return pl.pallas_call(
        finish_kernel,
        out_shape=jax.ShapeDtypeStruct((ROWS, 2 * HD), jnp.bfloat16),
        in_specs=[pl.BlockSpec(memory_space=pltpu.SMEM), vmem, vmem, vmem],
        out_specs=vmem,
        compiler_params=pltpu.CompilerParams(vmem_limit_bytes=VMEM_LIMIT),
    )(pos, own, from_core, from_face)


def arrange_kernel(pos_ref, mine_ref, other_ref, out_ref):
    time_pos, height_pos, width_pair, core = (pos_ref[i] for i in range(4))
    depth = mine_ref.shape[1]
    for flip_c, ref in enumerate((mine_ref, other_ref)):

        def one_block(at, _, ref=ref, flip_c=flip_c):
            t = time_pos ^ (2 * (at & 1)) ^ ((at >> 3) & 1)
            u = height_pos ^ ((at >> 1) & 1) ^ (3 * ((at >> 2) & 1))
            w = width_pair ^ ((at >> 4) & 1)
            to = ((t * 4 + u) * 2 + w) * 2 + (core ^ flip_c)
            out_ref[pl.ds(pl.multiple_of(to * depth, depth), depth), :] = ref[at]
            return 0

        lax.fori_loop(0, mine_ref.shape[0], one_block, 0, unroll=4)


def project_kernel(groups, pos_ref, rows_ref, mine_ref, other_ref, gate_ref, out_ref, weight_ref):
    arrange_kernel(pos_ref, mine_ref, other_ref, weight_ref)
    depth = rows_ref.shape[3]
    total = jnp.zeros(out_ref.shape, jnp.float32)
    for x in range(groups):
        for slot in range(2):
            start = (x * 2 + (slot ^ pos_ref[4])) * depth
            weight = weight_ref[pl.ds(pl.multiple_of(start, depth), depth), :]
            total += jnp.dot(rows_ref[x, slot], weight, preferred_element_type=jnp.float32)
    out_ref[...] = (total * gate_ref[...]).astype(jnp.bfloat16)


def project(pos, rows, mine, other, gate):
    vmem = pl.BlockSpec(memory_space=pltpu.VMEM)
    depth, width = 2 * mine.shape[0] * mine.shape[1], mine.shape[2]
    return pl.pallas_call(
        functools.partial(project_kernel, rows.shape[0]),
        out_shape=jax.ShapeDtypeStruct((rows.shape[2], width), jnp.bfloat16),
        in_specs=[pl.BlockSpec(memory_space=pltpu.SMEM), vmem, vmem, vmem, vmem],
        out_specs=vmem,
        scratch_shapes=[pltpu.VMEM((depth, width), mine.dtype)],
        compiler_params=pltpu.CompilerParams(vmem_limit_bytes=VMEM_LIMIT),
    )(pos, rows, mine, other, gate)


def after(value, other):
    return lax.optimization_barrier((value, other))[0]


def local(queries, key_rows, value_rows, extents, out_weight, gate_scale):
    pos = jnp.stack([lax.axis_index(a) for a in ("t", "u", "w", "c", "h")])

    own_kv = beside(key_rows, value_rows)
    up = swapped(own_kv, "u", 1)
    down = middle_swapped(own_kv, "u")
    facing = [(1, 2), (2, 1)]
    tiles_q = [
        queries,
        swapped(queries, "c", 1),
        lax.ppermute(queries, ("w", "c"), facing),
    ]
    weight = out_weight[None]
    weight = joined(weight, swapped(weight, "t", 2))

    down, tiles_q, weight = lax.optimization_barrier((down, tiles_q, weight))
    near = joined(own_kv, up, down)
    early = swapped(near, "t", 1)
    late = middle_swapped(near, "t")
    weight, near = lax.optimization_barrier((weight, near))
    weight_u = swapped(weight, "u", 1)
    state, all_q = attend(pos, extents, tiles_q, 0, 3, 0, near)
    weight = joined(weight, after(weight_u, state))
    state, weight = lax.optimization_barrier((state, weight))
    weight_u = swapped(weight, "u", 3)

    state = attend(pos, extents, all_q, 0, 3, 1, early, state)
    given = attend(pos, extents, all_q, 1, 3, 2, late, state)
    state, given, weight_u = lax.optimization_barrier((state, given, weight_u))
    from_core = swapped(given[:, :, :LANES], "c", 1)
    from_face = lax.ppermute(given[:, :, LANES:], ("w", "c"), facing)
    weight = joined(weight, weight_u)
    weight_t = swapped(weight, "t", 1)
    own = attend(pos, extents, all_q, 0, 1, 2, late, state)
    attended = finish(pos, own, after(from_core, own), from_face)

    across = swapped(attended, "h", 1)
    weight = joined(weight, after(weight_t, attended))
    weight_w = swapped(weight, "w", 1)
    rows = lax.all_gather(joined(attended[None], across[None]), "x", axis=0, tiled=False)
    weight = joined(weight, after(weight_w, rows))
    return project(pos, rows, weight, swapped(weight, "c", 1), gate_scale[None, :])


def solution(mesh):
    fine = Mesh(mesh.devices.reshape(4, 4, 2, 2, 4, 2), ROW_AXES + COL_AXES)
    in_specs = (
        P(ROW_AXES, COL_AXES),
        P(ROW_AXES, COL_AXES),
        P(ROW_AXES, COL_AXES),
        P(COL_AXES, None),
        P(ROW_AXES, COL_AXES),
        P(COL_AXES),
    )
    return jax.shard_map(
        local, mesh=fine, in_specs=in_specs, out_specs=P(ROW_AXES, COL_AXES), check_vma=False
    )
```
